512 devices in a mesh: pipe: 32 (over z, x_lo), section: 8 (over x_hi, y), tensor: 2 (over core).
Axes of the slice: x: 4 (x_hi: 2, x_lo: 2; x = x_hi * 2 + x_lo), y: 4, z: 16, core: 2. Of those that a mesh axis runs over, the one named last changes fastest.
Arguments:
- stashed: bfloat16 [32, 8, 4, 48, 6144], P('pipe', 'section', None, None, 'tensor'), may hold values from -6 to 6
- cotangent: bfloat16 [32, 8, 4, 48, 6144], P('pipe', 'section', None, None, 'tensor'), may hold values from -3 to 3
- down_weight: bfloat16 [12, 2, 3072, 128], P(None, 'tensor', 'pipe'), may hold values from -0.078125 to 0.078125
- up_weight: bfloat16 [12, 2, 3072, 128], P(None, 'tensor', 'pipe'), may hold values from -0.5 to 0.5
- layer_split: int32 [16, 8], replicated, may hold values from 1 to 2, as said below
- template_of: int32 [32], replicated, may hold values from 0 to 15
- mb_count: int32 [32], replicated, may hold values from 1 to 4, 80 in all
Outputs:
- grad_down: float32 [12, 2, 3072, 128], P(None, 'tensor', ('pipe', 'section'))
- grad_up: float32 [12, 2, 3072, 128], P(None, 'tensor', ('pipe', 'section'))
The draws below stay inside these ranges and needn't reach their ends.
Inputs may be any that keep to these rules, and one draw needn't show every extreme that they name: `layer_split`: each row gives the consecutive layers held by the 8 sections of a template, in section order, and sums to 12. The first mb_count[p] microbatch slots of relay p are live.
All inputs are finite; a program needn't handle non-finite values.
Results may differ from the reference program's by a relative error of at most 0.006.
Values may be sent and summed in bfloat16 or wider, within the bound.
A program may use at most 64 MiB of HBM per device.

```python
import math
import jax
import jax.numpy as jnp
import numpy as np
from jax import lax

D = 6144
R = 128
TEMPLATES = 16
MB_CAP = 4
MB_TOK = 48
PIPES = 32
SECTIONS = 8
HALVES = 2
LAYERS = 12
DH = 3072


def draw_layer_split(key, part):
    key = jax.random.fold_in(key, 11)
    pattern = jnp.concatenate([jnp.full((SECTIONS // 2,), 2, jnp.int32), jnp.ones((SECTIONS - SECTIONS // 2,), jnp.int32)])
    row_keys = jax.random.split(key, TEMPLATES)
    return jax.vmap(lambda row_key: jax.random.permutation(row_key, pattern))(row_keys).astype(jnp.int32)


def plant(entries, key, low, top_value):
    index_at = [jax.random.randint(jax.random.fold_in(key, axis), (), 0, length) for axis, length in enumerate(entries.shape)]
    main_axis = entries.shape.index(max(entries.shape))
    next_to = index_at[:main_axis] + [(index_at[main_axis] + 1) % entries.shape[main_axis]] + index_at[main_axis + 1:]
    return entries.at[tuple(index_at)].set(low).at[tuple(next_to)].set(top_value)


def levels(stream_key, extent, cuts, low, largest):
    level = 1.0
    for axis_at, shards_of in cuts:
        heights = jax.random.uniform(jax.random.fold_in(jax.random.fold_in(stream_key, 6), axis_at), (shards_of,), jnp.float32, low / len(cuts), largest / len(cuts))
        level = level * jnp.repeat(jnp.exp(heights), extent[axis_at] // shards_of).reshape((-1,) + (1,) * (len(extent) - 1 - axis_at))
    return level


def length_profile(number_of, total, limit, skew):
    loads = [(1 << 20) // math.isqrt(standing ** skew) + 1 for standing in range(2, number_of + 1)]
    surplus, counts = total - limit - (number_of - 1), [1] * (number_of - 1)
    while surplus > 0:
        candidates = [i for i in range(number_of - 1) if counts[i] < limit]
        mass, left = sum([loads[i] for i in candidates]), surplus
        for i in candidates:
            extra = min(limit - counts[i], max(1, left * loads[i] // mass), surplus)
            counts[i] = counts[i] + extra
            surplus = surplus - extra
    return np.array([limit] + counts)


def ragged_sizes(rng, number_of, total, reach, slope):
    if number_of == 2:
        one = jax.random.randint(rng, (), max(1, total - reach), min(reach, total - 1) + 1)
        return jnp.stack([one, total - one])
    tallies = jnp.asarray(length_profile(number_of, total, reach, slope), jnp.int32)
    twos = (number_of - 1) // 2
    donor, taker = tallies[1:1 + 2 * twos:2], tallies[2:2 + 2 * twos:2]
    slack = jnp.minimum(donor - 1, reach - taker)
    shifted = jax.random.randint(jax.random.fold_in(rng, 1), (twos,), 0, 1 << 20) % (slack + 1)
    tallies = tallies.at[1:1 + 2 * twos:2].set(donor - shifted).at[2:2 + 2 * twos:2].set(taker + shifted)
    return tallies[jax.random.permutation(jax.random.fold_in(rng, 2), number_of)]


def normal_values(own_key, dims, deviation, limit, pieces=(), dtype=jnp.bfloat16):
    entries = jax.random.normal(own_key, dims, jnp.float32) * deviation
    if len(pieces) > 0:
        entries = levels(own_key, dims, pieces, -0.22, 0.18) * entries
    return jnp.clip(entries, min=-limit, max=limit).astype(dtype)


def setup_inputs(seed: int = 0) -> dict:
    streams_of = jax.random.split(jax.random.key(seed), 8)
    stashed = normal_values(streams_of[0], (PIPES, SECTIONS, MB_CAP, MB_TOK, D), 1.0, 6.0, ((0, 32), (1, 8), (4, 2)))
    cotangent = normal_values(streams_of[1], (PIPES, SECTIONS, MB_CAP, MB_TOK, D), 0.5, 3.0, ((0, 32), (1, 8), (4, 2)))
    down_weight = normal_values(streams_of[2], (LAYERS, HALVES, DH, R), D ** -0.5, 0.078125, ((1, 2), (2, 32)))
    up_weight = normal_values(streams_of[3], (LAYERS, HALVES, DH, R), R ** -0.5, 0.5, ((1, 2), (2, 32)))
    layer_split = draw_layer_split(jax.random.fold_in(streams_of[7], 71), 0)
    template_of = plant(jax.random.randint(streams_of[5], (PIPES,), 0, TEMPLATES), jax.random.fold_in(streams_of[5], 1), 0, TEMPLATES - 1).astype(jnp.int32)
    mb_count = ragged_sizes(streams_of[6], PIPES, 5 * PIPES // 2, MB_CAP, 2).astype(jnp.int32)
    return dict(stashed=stashed, cotangent=cotangent, down_weight=down_weight, up_weight=up_weight, layer_split=layer_split, template_of=template_of, mb_count=mb_count)


gelu_scale = 0.7978845608028654
gelu_cubic = 0.044715


def gelu_value(values):
    inner = jnp.tanh(gelu_scale * (values + gelu_cubic * values * values * values))
    return 0.5 * values * (1.0 + inner)


def gelu_slope(values):
    inner = jnp.tanh(gelu_scale * (values + gelu_cubic * values * values * values))
    return 0.5 * (1.0 + inner) + 0.5 * values * (1.0 - inner * inner) * gelu_scale * (1.0 + 3.0 * gelu_cubic * values * values)


def matmul(left, right):
    return jnp.dot(left.astype(jnp.float32), right.astype(jnp.float32), preferred_element_type=jnp.float32)


def rounded(values):
    return lax.optimization_barrier(values.astype(jnp.bfloat16)).astype(jnp.float32)


def reference(stashed, cotangent, down_weight, up_weight, layer_split, template_of, mb_count):
    row_count = MB_CAP * MB_TOK
    down_full = down_weight.reshape(LAYERS, D, R)
    up_full = up_weight.reshape(LAYERS, D, R)
    chosen = layer_split[template_of]
    firsts = jnp.cumsum(chosen, axis=1) - chosen
    live_rows = (jnp.arange(row_count) // MB_TOK)[None, :] < mb_count[:, None]
    section_inputs = stashed.reshape(PIPES * SECTIONS, row_count, D)
    section_cotangents = cotangent.reshape(PIPES * SECTIONS, row_count, D)
    live_flat = jnp.repeat(live_rows, SECTIONS, axis=0)
    first_flat = firsts.reshape(PIPES * SECTIONS).astype(jnp.int32)
    count_flat = chosen.reshape(PIPES * SECTIONS).astype(jnp.int32)

    def visit(carry, element):
        sum_down, sum_up = carry
        inputs, incoming, live, first, count = element
        incoming = jnp.where(live[:, None], incoming, jnp.zeros_like(incoming))
        layer_zero = first
        layer_one = jnp.minimum(first + 1, LAYERS - 1)
        holds_two = count > 1
        pre_zero = matmul(inputs, down_full[layer_zero])
        act_zero = gelu_value(pre_zero).astype(jnp.bfloat16)
        input_one = (inputs.astype(jnp.float32) + matmul(act_zero, up_full[layer_zero].T)).astype(jnp.bfloat16)
        pre_one = matmul(input_one, down_full[layer_one])
        act_one = gelu_value(pre_one).astype(jnp.bfloat16)
        back_one = matmul(incoming, up_full[layer_one])
        slope_one = (back_one * gelu_slope(pre_one)).astype(jnp.bfloat16)
        term_down_one = rounded(matmul(input_one.T, slope_one))
        term_up_one = rounded(matmul(incoming.T, act_one))
        passed = (incoming.astype(jnp.float32) + matmul(slope_one, down_full[layer_one].T)).astype(jnp.bfloat16)
        cot_zero = jnp.where(holds_two, passed, incoming)
        back_zero = matmul(cot_zero, up_full[layer_zero])
        slope_zero = (back_zero * gelu_slope(pre_zero)).astype(jnp.bfloat16)
        term_down_zero = rounded(matmul(inputs.T, slope_zero))
        term_up_zero = rounded(matmul(cot_zero.T, act_zero))
        weight_one = jnp.where(holds_two, 1.0, 0.0).astype(jnp.float32)
        sum_down = sum_down.at[layer_zero].add(term_down_zero)
        sum_down = sum_down.at[layer_one].add(weight_one * term_down_one)
        sum_up = sum_up.at[layer_zero].add(term_up_zero)
        sum_up = sum_up.at[layer_one].add(weight_one * term_up_one)
        return (sum_down, sum_up), None

    start = (jnp.zeros((LAYERS, D, R), jnp.float32), jnp.zeros((LAYERS, D, R), jnp.float32))
    (sum_down, sum_up), _ = lax.scan(visit, start, (section_inputs, section_cotangents, live_flat, first_flat, count_flat))
    total_count = jnp.sum(mb_count).astype(jnp.float32)
    grad_down = (sum_down / total_count).reshape(LAYERS, HALVES, DH, R)
    grad_up = (sum_up / total_count).reshape(LAYERS, HALVES, DH, R)
    return (grad_down, grad_up)
```

```python
import jax
import jax.numpy as jnp
import numpy as np
from jax import lax
from jax.experimental import pallas as pl
from jax.experimental.pallas import tpu as pltpu
from jax.sharding import PartitionSpec as P

MESH = pl.DeviceIdType.MESH
F32 = jnp.float32
BF16 = jnp.bfloat16

LAYERS = 12
SECTIONS = 8
ZS = 16
SIDE = 4
PLANE = 16
ROWS = 192
HALF = 3072
UNIT = 16
CHUNK = 384
CHUNKS = HALF // CHUNK
SLAB = 48
VMEM_LIMIT = 50 * 2**20

OFFSETS = (
    (1, 0), (0, 1), (3, 0), (0, 3), (2, 0), (0, 2), (1, 1), (3, 3),
    (1, 3), (3, 1), (2, 1), (1, 2), (2, 3), (3, 2), (2, 2),
)

gelu_scale = 0.7978845608028654
gelu_cubic = 0.044715


def gelu_pair(values):
    inner = jnp.tanh(gelu_scale * (values + gelu_cubic * values * values * values))
    value = 0.5 * values * (1.0 + inner)
    slope = 0.5 * (1.0 + inner) + 0.5 * values * (1.0 - inner * inner) * gelu_scale * (
        1.0 + 3.0 * gelu_cubic * values * values
    )
    return value, slope


def place():
    pipe = lax.axis_index("pipe")
    section = lax.axis_index("section")
    z, x_lo = pipe // 2, pipe % 2
    x, y = (section // SIDE) * 2 + x_lo, section % SIDE
    return z, x, y, x_lo, section


def chip(z, x, y):
    return {"pipe": z * 2 + x % 2, "section": (x // 2) * SIDE + y}


def seat(x, y):
    return (x % 2) * SECTIONS + (x // 2) * SIDE + y


def plane_steps(x, y):
    core = lax.axis_index("tensor")
    for a, b in OFFSETS:
        yield (x + a + core * (b - a)) % SIDE, (y + b + core * (a - b)) % SIDE


def greet(z, x, y):
    barrier = pltpu.get_barrier_semaphore()
    for tx, ty in plane_steps(x, y):
        pl.semaphore_signal(barrier, inc=1, device_id=chip(z, tx, ty), device_id_type=MESH)
    for step in (1, ZS - 1):
        pl.semaphore_signal(
            barrier, inc=1, device_id=chip((z + step) % ZS, x, y), device_id_type=MESH
        )


def greeted():
    pl.semaphore_wait(pltpu.get_barrier_semaphore(), PLANE - 1 + 2)


def remote(src, dst, send_sem, recv_sem, target):
    return pltpu.make_async_remote_copy(
        src_ref=src, dst_ref=dst, send_sem=send_sem, recv_sem=recv_sem,
        device_id=target, device_id_type=MESH,
    )


def wait_bytes(ref, sem):
    pltpu.make_async_copy(ref, ref, sem).wait()


def share(section, z):
    return (section + 2 * (z % 4)) % 8


def weights_kernel(
    tmpl_ref, split_ref, down_ref, up_ref, got_ref,
    layer_at, ring, work, stage, ring_send, ring_recv, send_sem, recv_sem,
):
    z, x, y, x_lo, section = place()
    greet(z, x, y)
    for lo in range(2):
        template = tmpl_ref[2 * z + lo]
        first = jnp.int32(0)
        for s in range(SECTIONS):
            layer_at[(lo * SECTIONS + s) * 2] = first
            layer_at[(lo * SECTIONS + s) * 2 + 1] = jnp.minimum(first + 1, LAYERS - 1)
            first = first + split_ref[template, s]
    own = pl.ds(pl.multiple_of(jnp.minimum(share(section, z), 5) * UNIT, UNIT), UNIT)
    for layer in range(LAYERS):
        for way in range(2):
            ring[way, 0, layer] = down_ref[layer, own, :]
            ring[way, 0, LAYERS + layer] = up_ref[layer, own, :]
    greeted()
    me = seat(x, y)

    def carried(at):
        return share(section, at % ZS) < 6

    def ring_copy(way, step, half=None):
        part = slice(None) if half is None else pl.ds(half * LAYERS, LAYERS)
        return remote(
            ring.at[way, step - 1, part], ring.at[way, step, part],
            ring_send.at[way, step], ring_recv.at[way, step],
            chip((z + (1 if way == 0 else ZS - 1)) % ZS, x, y),
        )

    def back(way, step):
        return z - step + ZS if way == 0 else z + step

    def ring_start(step, halves=False):
        for way in range(2):
            @pl.when(carried(back(way, step - 1)))
            def _():
                ring_copy(way, step, way if halves else None).start()

    def ring_wait(step, halves=False):
        for way in range(2):
            @pl.when(carried(back(way, step)))
            def _():
                ring_copy(way, step, way if halves else None).wait_recv()

    def ring_sent(step, halves=False):
        for way in range(2):
            @pl.when(carried(back(way, step - 1)))
            def _():
                ring_copy(way, step, way if halves else None).wait_send()

    def hand_out(way, step, entry, last=False):
        at = back(way, step) % ZS

        @pl.when(carried(at))
        def _():
            if last:
                work[:LAYERS] = ring[0, step, :LAYERS]
                work[LAYERS:] = ring[1, step, LAYERS:]
            else:
                work[...] = ring[way, step]
            for target in range(PLANE):
                for slot in range(2):
                    layer = layer_at[target * 2 + slot]
                    stage[entry, target, slot] = work[layer]
                    stage[entry, target, 2 + slot] = work[LAYERS + layer]
            unit = (2 * at + x_lo) * 6 + share(section, at)
            got_ref[unit] = stage[entry, me]
            for tx, ty in plane_steps(x, y):
                remote(
                    stage.at[entry, seat(tx, ty)], got_ref.at[unit],
                    send_sem.at[entry], recv_sem.at[entry], chip(z, tx, ty),
                ).start()

    ring_start(1)
    hand_out(0, 0, 0)

    def middle(step, _):
        ring_wait(step)
        ring_start(step + 1)
        hand_out(0, step, 2 * step - 1)
        hand_out(1, step, 2 * step)
        return 0

    lax.fori_loop(1, 7, middle, 0)
    ring_wait(7)
    ring_start(8, True)
    hand_out(0, 7, 13)
    hand_out(1, 7, 14)
    ring_wait(8, True)
    hand_out(0, 8, 15, True)

    def finish(entry, _):
        step = (entry + 1) // 2
        at = jnp.where(entry % 2 == 1, z - step + ZS, z + step)

        @pl.when(carried(at))
        def _():
            wait_bytes(stage.at[entry, pl.ds(0, PLANE - 1)], send_sem.at[entry])
            wait_bytes(got_ref.at[pl.ds(0, 11)], recv_sem.at[entry])

        @pl.when(jnp.logical_not(carried(at)))
        def _():
            wait_bytes(got_ref.at[pl.ds(0, 12)], recv_sem.at[entry])

        return 0

    lax.fori_loop(0, ZS, finish, 0)

    def ring_finish(step, _):
        ring_sent(step)
        return 0

    lax.fori_loop(1, 8, ring_finish, 0)
    ring_sent(8, True)


def terms_kernel(
    tmpl_ref, split_ref, mb_ref, x_ref, cot_ref, got_ref, order_ref, out_ref,
    inc, input_one, cot_zero, turned, part, other, send_sem, recv_sem,
):
    pipe, section, core = lax.axis_index("pipe"), lax.axis_index("section"), lax.axis_index("tensor")
    barrier = pltpu.get_barrier_semaphore()
    pl.semaphore_signal(barrier, inc=1, device_id={"tensor": 1 - core}, device_id_type=MESH)
    live = mb_ref[pipe]
    holds_two = jnp.where(split_ref[tmpl_ref[pipe], section] > 1, 1.0, 0.0)

    def weight(kind, q):
        return got_ref[pl.ds(q * (CHUNK // UNIT), CHUNK // UNIT), kind].reshape(CHUNK, 128)

    def columns(q):
        return pl.ds(pl.multiple_of(q * CHUNK, CHUNK), CHUNK)

    def dot(a, b):
        return jnp.dot(a, b, preferred_element_type=F32)

    def dot_turned(a, b):
        return lax.dot_general(a, b, (((1,), (1,)), ((), ())), preferred_element_type=F32)

    def exchange(at, count):
        copy = remote(
            part.at[pl.ds(at, count)], other.at[pl.ds(at, count)],
            send_sem.at[at], recv_sem.at[at], {"tensor": 1 - core},
        )
        copy.start()
        copy.wait()
        return [part[at + i] + other[at + i] for i in range(count)]

    part[...] = jnp.zeros_like(part)

    def first(q, _):
        cols = columns(q)
        for m in range(4):
            keep = jnp.where(m < live, 1.0, 0.0)
            rows = pl.ds(m * SLAB, SLAB)
            inc[rows, cols] = (cot_ref[rows, cols].astype(F32) * keep).astype(BF16)
        part[0] += dot(x_ref[:, cols], weight(0, q))
        part[1] += dot(inc[:, cols], weight(3, q))
        return 0

    lax.fori_loop(0, CHUNKS, first, 0)
    pl.semaphore_wait(barrier, 1)
    pre_zero, back_one = exchange(0, 2)
    value, slope_at_zero = gelu_pair(pre_zero)
    act_zero = value.astype(BF16)
    act_zero_t = value.T.astype(BF16)

    def second(q, _):
        cols = columns(q)
        moved = x_ref[:, cols].astype(F32) + dot_turned(act_zero, weight(2, q))
        rounded = moved.astype(BF16)
        input_one[:, cols] = rounded
        part[2] += dot(rounded, weight(1, q))
        return 0

    lax.fori_loop(0, CHUNKS, second, 0)
    (pre_one,) = exchange(2, 1)
    value, slope = gelu_pair(pre_one)
    act_one_t = value.T.astype(BF16)
    slope_one_wide = back_one * slope * holds_two
    slope_one = slope_one_wide.astype(BF16)
    slope_one_t = slope_one_wide.T.astype(BF16)

    def third(q, _):
        cols = columns(q)
        moved = inc[:, cols].astype(F32) + dot_turned(slope_one, weight(1, q))
        rounded = moved.astype(BF16)
        cot_zero[:, cols] = rounded
        part[3] += dot(rounded, weight(2, q))
        turned[q, 128:, :CHUNK] = dot(slope_one_t, input_one[:, cols]).astype(BF16)
        turned[q, 128:, CHUNK:] = dot(act_one_t, inc[:, cols]).astype(BF16)
        return 0

    lax.fori_loop(0, CHUNKS, third, 0)
    (back_zero,) = exchange(3, 1)
    slope_zero_t = (back_zero * slope_at_zero).T.astype(BF16)

    def fourth(q, _):
        cols = columns(q)
        turned[q, :128, :CHUNK] = dot(slope_zero_t, x_ref[:, cols]).astype(BF16)
        turned[q, :128, CHUNK:] = dot(act_zero_t, cot_zero[:, cols]).astype(BF16)
        sorted_rows = dot_turned(order_ref[...], turned[q]).astype(BF16)
        for slot in range(2):
            out_ref[q, :, slot] = sorted_rows[:, slot * 128:(slot + 1) * 128].reshape(PLANE, SLAB, 128)
        return 0

    lax.fori_loop(0, CHUNKS, fourth, 0)


GROUPS = ((4,), (3, 5), (2, 6), (1, 7), (0,))
RUNS = ((1,), (2, 3), (4, 5), (6, 7), (8,))
BLOCK = LAYERS * 24


def sums_kernel(
    tmpl_ref, split_ref, mb_ref, terms_ref, down_ref, up_ref,
    source, landed, work, table, going, coming, total,
    send_sem, recv_sem, ring_send, ring_recv,
):
    z, x, y, x_lo, section = place()
    greet(z, x, y)
    me = seat(x, y)
    for lo in range(2):
        template = tmpl_ref[2 * z + lo]
        firsts = []
        first = jnp.int32(0)
        for s in range(SECTIONS):
            firsts.append(first)
            first = first + split_ref[template, s]
        for layer in range(LAYERS):
            at, begins = jnp.int32(0), jnp.int32(0)
            for s in range(1, SECTIONS):
                at = jnp.where(firsts[s] <= layer, s, at)
                begins = jnp.where(firsts[s] <= layer, firsts[s], begins)
            slot = jnp.minimum(layer - begins, 1)
            source[lo * LAYERS + layer] = (lo * SECTIONS + at) * 2 + slot
    count = jnp.int32(0)
    for relay in range(2 * ZS):
        count = count + mb_ref[relay]
    greeted()

    def chunk_of(shift):
        return (z // 2 + shift) % CHUNKS

    def send_group(group):
        for tx, ty in plane_steps(x, y):
            for shift in group:
                q = chunk_of(shift)
                remote(
                    terms_ref.at[q, seat(tx, ty)], landed.at[q, me],
                    send_sem.at[shift], recv_sem.at[shift], chip(z, tx, ty),
                ).start()

    def add_up(shift):
        q = chunk_of(shift)
        landed[q, me] = terms_ref[q, me]
        wait_bytes(landed.at[q, pl.ds(0, PLANE - 1)], recv_sem.at[shift])
        work[...] = landed[q].reshape(2 * PLANE, SLAB, 128)
        for layer in range(LAYERS):
            both = work[source[layer]].astype(F32) + work[source[LAYERS + layer]].astype(F32)
            rows = pl.ds(layer * 24, 24)
            table[2 * q, rows] = both[:24]
            table[2 * q + 1, rows] = both[24:]

    HALF_BLOCK = BLOCK // 2

    def ring_copy(way, step):
        part = pl.ds(way * HALF_BLOCK, HALF_BLOCK) if step == 1 else slice(None)
        return remote(
            going.at[way, step - 1, part], coming.at[way, step - 1, part],
            ring_send.at[way, step - 1], ring_recv.at[way, step - 1],
            chip((z + (1 if way == 0 else ZS - 1)) % ZS, x, y),
        )

    def ring_step(step):
        far = 9 - step
        for way in range(2):
            to = (z + (far if way == 0 else ZS - far)) % ZS
            mine = pl.ds(way * HALF_BLOCK, HALF_BLOCK)
            if step == 1:
                going[way, 0, mine] = table[to, mine].astype(BF16)
            else:
                ring_copy(way, step - 1).wait_recv()
                if step == 2:
                    rest = pl.ds((1 - way) * HALF_BLOCK, HALF_BLOCK)
                    going[way, 1, mine] = (
                        table[to, mine] + coming[way, 0, mine].astype(F32)
                    ).astype(BF16)
                    going[way, 1, rest] = table[to, rest].astype(BF16)
                else:
                    going[way, step - 1] = (
                        table[to] + coming[way, step - 2].astype(F32)
                    ).astype(BF16)
            ring_copy(way, step).start()

    send_group(GROUPS[0])
    send_group(GROUPS[1])
    for turn, group in enumerate(GROUPS):
        for shift in group:
            add_up(shift)
        if turn + 2 < len(GROUPS):
            send_group(GROUPS[turn + 2])
        for step in RUNS[turn]:
            ring_step(step)
    ring_copy(0, 8).wait_recv()
    ring_copy(1, 8).wait_recv()
    scale = count.astype(F32)
    total[...] = (table[z] + coming[0, 7].astype(F32) + coming[1, 7].astype(F32)) / scale
    for layer in range(LAYERS):
        down_ref[layer] = total[layer * 24:layer * 24 + 12]
        up_ref[layer] = total[layer * 24 + 12:layer * 24 + 24]
    for step in range(1, 9):
        for way in range(2):
            ring_copy(way, step).wait_send()
    for shift in range(CHUNKS):
        wait_bytes(terms_ref.at[chunk_of(shift), pl.ds(0, PLANE - 1)], send_sem.at[shift])


def row_order():
    order = np.zeros((768, 768), np.float32)
    for lo in range(2):
        for s in range(SECTIONS):
            for near in range(2):
                for kind in range(2):
                    for j in range(12):
                        to = lo * 384 + s * 48 + near * 24 + kind * 12 + j
                        order[to, kind * 384 + (2 * near + lo) * 96 + s * 12 + j] = 1.0
    return order


def call(kernel, number, out_shape, spaces, scratch, *operands):
    many = isinstance(out_shape, (list, tuple))
    vmem = pl.BlockSpec(memory_space=pltpu.VMEM)
    return pl.pallas_call(
        kernel,
        out_shape=out_shape,
        in_specs=[pl.BlockSpec(memory_space=space) for space in spaces],
        out_specs=[vmem] * len(out_shape) if many else vmem,
        scratch_shapes=scratch,
        compiler_params=pltpu.CompilerParams(
            collective_id=number, has_side_effects=True, vmem_limit_bytes=VMEM_LIMIT
        ),
    )(*operands)


def local(stashed, cotangent, down_weight, up_weight, layer_split, template_of, mb_count):
    smem, vmem = pltpu.SMEM, pltpu.VMEM
    dma = pltpu.SemaphoreType.DMA
    got = call(
        weights_kernel, 1,
        jax.ShapeDtypeStruct((HALF // UNIT, 4, UNIT, 128), BF16),
        (smem, smem, vmem, vmem),
        [
            pltpu.SMEM((2 * PLANE,), jnp.int32),
            pltpu.VMEM((2, 9, 2 * LAYERS, UNIT, 128), BF16),
            pltpu.VMEM((2 * LAYERS, UNIT, 128), BF16),
            pltpu.VMEM((ZS, PLANE, 4, UNIT, 128), BF16),
            dma((2, 9)), dma((2, 9)), dma((ZS,)), dma((ZS,)),
        ],
        template_of, layer_split, down_weight[:, 0], up_weight[:, 0],
    )
    order = jnp.asarray(row_order(), BF16)
    terms = call(
        terms_kernel, 2,
        jax.ShapeDtypeStruct((CHUNKS, PLANE, 2, SLAB, 128), BF16),
        (smem, smem, smem, vmem, vmem, vmem, vmem),
        [
            pltpu.VMEM((ROWS, HALF), BF16),
            pltpu.VMEM((ROWS, HALF), BF16),
            pltpu.VMEM((ROWS, HALF), BF16),
            pltpu.VMEM((CHUNKS, 256, 2 * CHUNK), BF16),
            pltpu.VMEM((4, ROWS, 128), F32),
            pltpu.VMEM((4, ROWS, 128), F32),
            dma((4,)), dma((4,)),
        ],
        template_of, layer_split, mb_count,
        stashed.reshape(ROWS, HALF), cotangent.reshape(ROWS, HALF), got, order,
    )
    grad = jax.ShapeDtypeStruct((LAYERS, 12, 128), F32)
    grad_down, grad_up = call(
        sums_kernel, 3,
        [grad, grad],
        (smem, smem, smem, vmem),
        [
            pltpu.SMEM((2 * LAYERS,), jnp.int32),
            pltpu.VMEM((CHUNKS, PLANE, 2, SLAB, 128), BF16),
            pltpu.VMEM((2 * PLANE, SLAB, 128), BF16),
            pltpu.VMEM((ZS, BLOCK, 128), F32),
            pltpu.VMEM((2, 8, BLOCK, 128), BF16),
            pltpu.VMEM((2, 8, BLOCK, 128), BF16),
            pltpu.VMEM((BLOCK, 128), F32),
            dma((CHUNKS,)), dma((CHUNKS,)), dma((2, 8)), dma((2, 8)),
        ],
        template_of, layer_split, mb_count, terms,
    )
    return grad_down[:, None], grad_up[:, None]


def solution(mesh):
    placed = (
        P("pipe", "section", None, None, "tensor"),
        P("pipe", "section", None, None, "tensor"),
        P(None, "tensor", "pipe", None),
        P(None, "tensor", "pipe", None),
        P(),
        P(),
        P(),
    )
    return jax.shard_map(
        local,
        mesh=mesh,
        in_specs=placed,
        out_specs=(
            P(None, "tensor", ("pipe", "section"), None),
            P(None, "tensor", ("pipe", "section"), None),
        ),
        check_vma=False,
    )
```

```python
import jax
import jax.numpy as jnp
import numpy as np
from jax import lax
from jax.experimental import pallas as pl
from jax.experimental.pallas import tpu as pltpu
from jax.sharding import PartitionSpec as P

MESH = pl.DeviceIdType.MESH
F32 = jnp.float32
BF16 = jnp.bfloat16

LAYERS = 12
SECTIONS = 8
ZS = 16
SIDE = 4
PLANE = 16
ROWS = 192
HALF = 3072
UNIT = 16
CHUNK = 384
CHUNKS = HALF // CHUNK
SLAB = 48
VMEM_LIMIT = 56 * 2**20

OFFSETS = (
    (1, 0), (0, 1), (3, 0), (0, 3), (2, 0), (0, 2), (1, 1), (3, 3),
    (1, 3), (3, 1), (2, 1), (1, 2), (2, 3), (3, 2), (2, 2),
)

gelu_scale = 0.7978845608028654
gelu_cubic = 0.044715


def gelu_pair(values):
    inner = jnp.tanh(gelu_scale * (values + gelu_cubic * values * values * values))
    value = 0.5 * values * (1.0 + inner)
    slope = 0.5 * (1.0 + inner) + 0.5 * values * (1.0 - inner * inner) * gelu_scale * (
        1.0 + 3.0 * gelu_cubic * values * values
    )
    return value, slope


def place():
    pipe = lax.axis_index("pipe")
    section = lax.axis_index("section")
    z, x_lo = pipe // 2, pipe % 2
    x, y = (section // SIDE) * 2 + x_lo, section % SIDE
    return z, x, y, x_lo, section


def chip(z, x, y):
    return {"pipe": z * 2 + x % 2, "section": (x // 2) * SIDE + y}


def seat(x, y):
    return (x % 2) * SECTIONS + (x // 2) * SIDE + y


def plane_steps(x, y):
    core = lax.axis_index("tensor")
    for a, b in OFFSETS:
        yield (x + a + core * (b - a)) % SIDE, (y + b + core * (a - b)) % SIDE


def remote(src, dst, send_sem, recv_sem, target):
    return pltpu.make_async_remote_copy(
        src_ref=src, dst_ref=dst, send_sem=send_sem, recv_sem=recv_sem,
        device_id=target, device_id_type=MESH,
    )


def wait_bytes(ref, sem):
    pltpu.make_async_copy(ref, ref, sem).wait()


def share(section, z):
    return (section + 2 * (z % 4)) % 8


def dot(a, b):
    return jnp.dot(a, b, preferred_element_type=F32)


def dot_turned(a, b):
    return lax.dot_general(a, b, (((1,), (1,)), ((), ())), preferred_element_type=F32)


LAST = 15
BLOCK = LAYERS * 24
HALF_BLOCK = BLOCK // 2
HALF_LAYERS = LAYERS // 2


def kernel(
    tmpl_ref, split_ref, mb_ref, x_hbm, cot_hbm, down_hbm, up_hbm, order_hbm, grad_down_ref, grad_up_ref,
    layer_at, source, x_ref, cot_ref, order_ref, blocks, work, stage, got,
    inc, input_one, cot_zero, turned, part, other, terms, landed, gathered, table,
    far_go, near_go, far_in, near_in, total,
    local_sem, z_send, z_recv, hand_send, hand_recv, pair_send, pair_recv,
    term_send, term_recv, sum_send, sum_recv,
):
    z, x, y, x_lo, section = place()
    core = lax.axis_index("tensor")
    me = seat(x, y)
    odd = z % 2
    targets = [(seat(tx, ty), chip(z, tx, ty)) for tx, ty in plane_steps(x, y)]

    def column(step):
        return chip((z + step + 2 * ZS) % ZS, x, y)

    pair = {"tensor": 1 - core}
    barrier = pltpu.get_barrier_semaphore()
    for _, device in targets:
        pl.semaphore_signal(barrier, inc=1, device_id=device, device_id_type=MESH)
    for step in (1, -1, 2, -2):
        pl.semaphore_signal(barrier, inc=1, device_id=column(step), device_id_type=MESH)
    pl.semaphore_signal(barrier, inc=1, device_id=pair, device_id_type=MESH)

    own = pl.ds(pl.multiple_of(jnp.minimum(share(section, z), 5) * UNIT, UNIT), UNIT)
    loads = [
        pltpu.make_async_copy(down_hbm.at[:, own], blocks.at[0, :, 0], local_sem.at[0]),
        pltpu.make_async_copy(up_hbm.at[:, own], blocks.at[0, :, 1], local_sem.at[1]),
        pltpu.make_async_copy(x_hbm, x_ref, local_sem.at[2]),
        pltpu.make_async_copy(cot_hbm, cot_ref, local_sem.at[3]),
        pltpu.make_async_copy(order_hbm, order_ref, local_sem.at[4]),
    ]
    for load in loads:
        load.start()

    loads[0].wait()
    loads[1].wait()
    pl.semaphore_wait(barrier, PLANE - 1 + 4 + 1)

    def carried(at):
        return share(section, at % ZS) < 6

    def behind(way, distance):
        return (z + ZS - distance) % ZS if way == 0 else (z + distance) % ZS

    def entry_at(way, distance):
        if isinstance(distance, int) and distance in (0, 8):
            return 0 if distance == 0 else LAST
        return jnp.where(distance == 0, 0, 2 * distance - 1 + way)

    def z_copy(way, step, half):
        part = pl.ds(half * HALF_LAYERS, HALF_LAYERS)
        return remote(
            blocks.at[entry_at(way, step - 1), part], blocks.at[entry_at(way, step), part],
            z_send.at[step, way, half], z_recv.at[step, way, half], column(1 if way == 0 else -1),
        )

    def z_each(step, half, action, arriving):
        for way in range(2):
            if isinstance(step, int) and step == 8 and way != half:
                continue

            @pl.when(carried(behind(way, step if arriving else step - 1)))
            def _():
                action(z_copy(way, step, half))

    def z_start(step, half):
        z_each(step, half, lambda copy: copy.start(), False)

    def z_arrived(step, half):
        z_each(step, half, lambda copy: copy.wait_recv(), True)

    def z_sent(step):
        for half in range(2):
            z_each(step, half, lambda copy: copy.wait_send(), False)

    def place_of(entry):
        distance = (entry + 1) // 2
        return jnp.where(entry % 2 == 1, z + ZS - distance, z + distance) % ZS

    def hand_out(entry):
        at = place_of(entry)

        @pl.when(carried(at))
        def _():
            work[...] = blocks[entry]
            for four in range(0, PLANE, 4):
                slots = [(target, slot) for target in range(four, four + 4) for slot in range(2)]
                cut = [work[layer_at[target * 2 + slot]] for target, slot in slots]
                for (target, slot), rows in zip(slots, cut):
                    stage[entry, target, slot] = rows
            unit = (2 * at + x_lo) * 6 + share(section, at)
            got[unit] = stage[entry, me]
            for where, device in targets:
                remote(
                    stage.at[entry, where], got.at[unit], hand_send.at[entry], hand_recv.at[entry], device
                ).start()

    def handed(entry):
        at = place_of(entry)

        @pl.when(carried(at))
        def _():
            wait_bytes(got.at[pl.ds(0, 11)], hand_recv.at[entry])

        @pl.when(jnp.logical_not(carried(at)))
        def _():
            wait_bytes(got.at[pl.ds(0, 12)], hand_recv.at[entry])

    def over(first, last, body):
        def step(index, _):
            body(index)
            return 0

        lax.fori_loop(first, last, step, 0)

    def chunk_of(m, side):
        return (z // 2 + odd + jnp.where(side == 0, m - 1, CHUNKS - m)) % CHUNKS

    def weight(slot, kind, q):
        return got[pl.ds(q * (CHUNK // UNIT), CHUNK // UNIT), slot, kind].reshape(CHUNK, 128)

    def columns(q):
        return pl.ds(pl.multiple_of(q * CHUNK, CHUNK), CHUNK)

    def begin(q):
        cols = columns(q)
        for m in range(4):
            keep = jnp.where(m < live, 1.0, 0.0)
            rows = pl.ds(m * SLAB, SLAB)
            inc[rows, cols] = (cot_ref[rows, cols].astype(F32) * keep).astype(BF16)
        part[0] += dot(x_ref[:, cols], weight(0, 0, q))
        part[1] += dot(inc[:, cols], weight(1, 1, q))

    for half in range(2):
        z_start(1, half)
    for lo in range(2):
        template = tmpl_ref[2 * z + lo]
        firsts = []
        first = jnp.int32(0)
        for s in range(SECTIONS):
            firsts.append(first)
            layer_at[(lo * SECTIONS + s) * 2] = jnp.minimum(first, LAYERS - 1)
            layer_at[(lo * SECTIONS + s) * 2 + 1] = jnp.minimum(first + 1, LAYERS - 1)
            first = first + split_ref[s, template]
        for layer in range(LAYERS):
            at, begins = jnp.int32(0), jnp.int32(0)
            for s in range(1, SECTIONS):
                at = jnp.where(firsts[s] <= layer, s, at)
                begins = jnp.where(firsts[s] <= layer, firsts[s], begins)
            slot = jnp.minimum(layer - begins, 1)
            source[lo * LAYERS + layer] = slot * PLANE + lo * SECTIONS + at
    live = mb_ref[2 * z + x_lo]
    holds_two = jnp.where(split_ref[section, tmpl_ref[2 * z + x_lo]] > 1, 1.0, 0.0)
    count = jnp.int32(0)
    for relay in range(2 * ZS):
        count = count + mb_ref[relay]

    hand_out(jnp.int32(0))

    def ring_step(step):
        for half in range(2):
            z_arrived(step, half)
            z_start(step + 1, half)
        hand_out(2 * step - 1)
        hand_out(2 * step)

    over(1, 7, ring_step)
    for half in range(2):
        z_arrived(7, half)
        z_start(8, half)
    hand_out(jnp.int32(13))
    hand_out(jnp.int32(14))
    for half in range(2):
        z_arrived(8, half)
    hand_out(jnp.int32(15))

    part[...] = jnp.zeros_like(part)
    for load in loads[2:]:
        load.wait()
    for m in range(1, 5):
        over(0 if m == 1 else 4 * m - 3, min(4 * m + 1, ZS), handed)
        over(0, 2, lambda side: begin(chunk_of(m, side)))

    def exchange(at, number):
        copy = remote(
            part.at[pl.ds(at, number)], other.at[pl.ds(at, number)], pair_send.at[at], pair_recv.at[at], pair
        )
        copy.start()
        copy.wait()
        return [part[at + i] + other[at + i] for i in range(number)]

    pre_zero, back_one = exchange(0, 2)
    value, slope_at_zero = gelu_pair(pre_zero)
    act_zero = value.astype(BF16)
    act_zero_t = value.T.astype(BF16)

    def second(q):
        cols = columns(q)
        moved = x_ref[:, cols].astype(F32) + dot_turned(act_zero, weight(0, 1, q))
        rounded = moved.astype(BF16)
        input_one[:, cols] = rounded
        part[2] += dot(rounded, weight(1, 0, q))

    over(0, CHUNKS, second)
    (pre_one,) = exchange(2, 1)
    value, slope = gelu_pair(pre_one)
    act_one_t = value.T.astype(BF16)
    slope_one_wide = back_one * slope * holds_two
    slope_one = slope_one_wide.astype(BF16)
    slope_one_t = slope_one_wide.T.astype(BF16)

    def give(slot, q):
        sorted_rows = dot_turned(order_ref[...], turned[...]).astype(BF16)
        terms[slot, q] = sorted_rows.reshape(PLANE, SLAB, 128)
        for where, device in targets:
            remote(
                terms.at[slot, q, where], landed.at[slot, q, me],
                term_send.at[slot, q], term_recv.at[slot, q], device,
            ).start()

    def third(step):
        q = chunk_of(4 - step // 2, step % 2)
        cols = columns(q)
        turned[:, :CHUNK] = dot(slope_one_t, input_one[:, cols]).astype(BF16)
        turned[:, CHUNK:] = dot(act_one_t, inc[:, cols]).astype(BF16)
        give(1, q)
        moved = inc[:, cols].astype(F32) + dot_turned(slope_one, weight(1, 0, q))
        rounded = moved.astype(BF16)
        cot_zero[:, cols] = rounded
        part[3] += dot(rounded, weight(0, 1, q))

    over(0, CHUNKS, third)
    (back_zero,) = exchange(3, 1)
    slope_zero_t = (back_zero * slope_at_zero).T.astype(BF16)

    def fourth(q):
        cols = columns(q)
        turned[:, :CHUNK] = dot(slope_zero_t, x_ref[:, cols]).astype(BF16)
        turned[:, CHUNK:] = dot(act_zero_t, cot_zero[:, cols]).astype(BF16)
        give(0, q)

    def add_up(q):
        for slot in range(2):
            landed[slot, q, me] = terms[slot, q, me]
            wait_bytes(landed.at[slot, q, pl.ds(0, PLANE - 1)], term_recv.at[slot, q])
            gathered[slot * PLANE:(slot + 1) * PLANE] = landed[slot, q]
        for two in range(0, LAYERS, 2):
            both = [
                gathered[source[layer]].astype(F32) + gathered[source[LAYERS + layer]].astype(F32)
                for layer in (two, two + 1)
            ]
            for layer, rows in zip((two, two + 1), both):
                table[2 * q, pl.ds(layer * 24, 24)] = rows[:24]
                table[2 * q + 1, pl.ds(layer * 24, 24)] = rows[24:]

    def sum_copy(m, far, way):
        i = 4 - m
        step = (1 + far) * (1 if way == 0 else -1)
        if not far:
            return remote(
                near_go.at[way, i], near_in.at[way, i], sum_send.at[way, i, 0], sum_recv.at[way, i, 0], column(step)
            )
        rows = pl.ds(way * HALF_BLOCK, HALF_BLOCK) if m == 4 else slice(None)
        return remote(
            far_go.at[way, i, rows], far_in.at[way, i, rows], sum_send.at[way, i, 1], sum_recv.at[way, i, 1], column(step)
        )

    def pass_on(m):
        i = 4 - m
        for way in range(2):
            near_go[way, i] = table[behind(1 - way, 2 * m - 1)].astype(BF16)
            sum_copy(m, 0, way).start()
        for way in range(2):
            to = behind(1 - way, 2 * m)
            mine = pl.ds(way * HALF_BLOCK, HALF_BLOCK)
            rest = pl.ds((1 - way) * HALF_BLOCK, HALF_BLOCK)
            if m == 4:
                far_go[way, 0, mine] = table[to, mine].astype(BF16)
            else:
                sum_copy(m + 1, 0, way).wait_recv()
                sum_copy(m + 1, 1, way).wait_recv()
                if m == 3:
                    far_go[way, 1, mine] = (
                        table[to, mine] + near_in[way, 0, mine].astype(F32) + far_in[way, 0, mine].astype(F32)
                    ).astype(BF16)
                    far_go[way, 1, rest] = (table[to, rest] + near_in[way, 0, rest].astype(F32)).astype(BF16)
                else:
                    far_go[way, i] = (
                        table[to] + near_in[way, i - 1].astype(F32) + far_in[way, i - 1].astype(F32)
                    ).astype(BF16)
            sum_copy(m, 1, way).start()

    over(0, 2, lambda side: fourth(chunk_of(4, side)))
    for m in range(4, 0, -1):
        if m > 1:
            over(0, 2, lambda side: fourth(chunk_of(m - 1, side)))
        over(0, 2, lambda side: add_up(chunk_of(m, side)))
        pass_on(m)
    result = table[z]
    for way in range(2):
        sum_copy(1, 0, way).wait_recv()
        sum_copy(1, 1, way).wait_recv()
        result = result + near_in[way, 3].astype(F32) + far_in[way, 3].astype(F32)
    total[...] = result / count.astype(F32)
    for layer in range(LAYERS):
        grad_down_ref[layer * 12:layer * 12 + 12] = total[layer * 24:layer * 24 + 12]
        grad_up_ref[layer * 12:layer * 12 + 12] = total[layer * 24 + 12:layer * 24 + 24]

    over(1, 8, z_sent)
    z_sent(8)
    for m in range(1, 5):
        for way in range(2):
            sum_copy(m, 0, way).wait_send()
            sum_copy(m, 1, way).wait_send()

    def left(entry):
        @pl.when(carried(place_of(entry)))
        def _():
            wait_bytes(stage.at[entry, pl.ds(0, PLANE - 1)], hand_send.at[entry])

    over(0, LAST + 1, left)

    def given(step):
        wait_bytes(terms.at[step // CHUNKS, step % CHUNKS, pl.ds(0, PLANE - 1)], term_send.at[step // CHUNKS, step % CHUNKS])

    over(0, 2 * CHUNKS, given)


def row_order():
    order = np.zeros((768, 768), np.float32)
    for lo in range(2):
        for s in range(SECTIONS):
            for near in range(2):
                for kind in range(2):
                    for j in range(12):
                        to = lo * 384 + s * 48 + near * 24 + kind * 12 + j
                        order[to, kind * 384 + (2 * near + lo) * 96 + s * 12 + j] = 1.0
    return order


def local(stashed, cotangent, down_weight, up_weight, layer_split, template_of, mb_count):
    smem, hbm = pl.BlockSpec(memory_space=pltpu.SMEM), pl.BlockSpec(memory_space=pl.ANY)
    dma = pltpu.SemaphoreType.DMA
    grad = jax.ShapeDtypeStruct((LAYERS * 12, 128), F32)
    grad_down, grad_up = pl.pallas_call(
        kernel,
        out_shape=[grad, grad],
        in_specs=[smem] * 3 + [hbm] * 5,
        out_specs=[pl.BlockSpec(memory_space=pltpu.VMEM)] * 2,
        scratch_shapes=[
            pltpu.SMEM((2 * PLANE,), jnp.int32),
            pltpu.SMEM((2 * LAYERS,), jnp.int32),
            pltpu.VMEM((ROWS, HALF), BF16),
            pltpu.VMEM((ROWS, HALF), BF16),
            pltpu.VMEM((768, 768), BF16),
            pltpu.VMEM((ZS, LAYERS, 2, UNIT, 128), BF16),
            pltpu.VMEM((LAYERS, 2, UNIT, 128), BF16),
            pltpu.VMEM((ZS, PLANE, 2, 2, UNIT, 128), BF16),
            pltpu.VMEM((HALF // UNIT, 2, 2, UNIT, 128), BF16),
            pltpu.VMEM((ROWS, HALF), BF16),
            pltpu.VMEM((ROWS, HALF), BF16),
            pltpu.VMEM((ROWS, HALF), BF16),
            pltpu.VMEM((128, 2 * CHUNK), BF16),
            pltpu.VMEM((4, ROWS, 128), F32),
            pltpu.VMEM((4, ROWS, 128), F32),
            pltpu.VMEM((2, CHUNKS, PLANE, SLAB, 128), BF16),
            pltpu.VMEM((2, CHUNKS, PLANE, SLAB, 128), BF16),
            pltpu.VMEM((2 * PLANE, SLAB, 128), BF16),
            pltpu.VMEM((ZS, BLOCK, 128), F32),
            pltpu.VMEM((2, 4, BLOCK, 128), BF16),
            pltpu.VMEM((2, 4, BLOCK, 128), BF16),
            pltpu.VMEM((2, 4, BLOCK, 128), BF16),
            pltpu.VMEM((2, 4, BLOCK, 128), BF16),
            pltpu.VMEM((BLOCK, 128), F32),
            dma((5,)), dma((9, 2, 2)), dma((9, 2, 2)), dma((ZS,)), dma((ZS,)), dma((4,)), dma((4,)),
            dma((2, CHUNKS)), dma((2, CHUNKS)), dma((2, 4, 2)), dma((2, 4, 2)),
        ],
        compiler_params=pltpu.CompilerParams(
            collective_id=1, has_side_effects=True, vmem_limit_bytes=VMEM_LIMIT
        ),
    )(
        template_of, layer_split.T, mb_count, stashed.reshape(ROWS, HALF), cotangent.reshape(ROWS, HALF),
        down_weight[:, 0], up_weight[:, 0], jnp.asarray(row_order(), BF16),
    )
    return grad_down.reshape(LAYERS, 1, 12, 128), grad_up.reshape(LAYERS, 1, 12, 128)


def solution(mesh):
    placed = (
        P("pipe", "section", None, None, "tensor"),
        P("pipe", "section", None, None, "tensor"),
        P(None, "tensor", "pipe", None),
        P(None, "tensor", "pipe", None),
        P(),
        P(),
        P(),
    )
    return jax.shard_map(
        local,
        mesh=mesh,
        in_specs=placed,
        out_specs=(
            P(None, "tensor", ("pipe", "section"), None),
            P(None, "tensor", ("pipe", "section"), None),
        ),
        check_vma=False,
    )
```

```python
import jax
import jax.numpy as jnp
import numpy as np
from jax import lax
from jax.experimental import pallas as pl
from jax.experimental.pallas import tpu as pltpu
from jax.sharding import PartitionSpec as P

MESH = pl.DeviceIdType.MESH
F32 = jnp.float32
BF16 = jnp.bfloat16

LAYERS = 12
SECTIONS = 8
ZS = 16
SIDE = 4
PLANE = 16
ROWS = 192
HALF = 3072
UNIT = 16
CHUNK = 384
CHUNKS = HALF // CHUNK
SLAB = 48
VMEM_LIMIT = 56 * 2**20

OFFSETS = (
    (1, 0), (0, 1), (3, 0), (0, 3), (2, 0), (0, 2), (1, 1), (3, 3),
    (1, 3), (3, 1), (2, 1), (1, 2), (2, 3), (3, 2), (2, 2),
)

gelu_scale = 0.7978845608028654
gelu_cubic = 0.044715


def gelu_pair(values):
    inner = jnp.tanh(gelu_scale * (values + gelu_cubic * values * values * values))
    value = 0.5 * values * (1.0 + inner)
    slope = 0.5 * (1.0 + inner) + 0.5 * values * (1.0 - inner * inner) * gelu_scale * (
        1.0 + 3.0 * gelu_cubic * values * values
    )
    return value, slope


def place():
    pipe = lax.axis_index("pipe")
    section = lax.axis_index("section")
    z, x_lo = pipe // 2, pipe % 2
    x, y = (section // SIDE) * 2 + x_lo, section % SIDE
    return z, x, y, x_lo, section


def chip(z, x, y):
    return {"pipe": z * 2 + x % 2, "section": (x // 2) * SIDE + y}


def seat(x, y):
    return (x % 2) * SECTIONS + (x // 2) * SIDE + y


def plane_steps(x, y):
    core = lax.axis_index("tensor")
    for a, b in OFFSETS:
        yield (x + a + core * (b - a)) % SIDE, (y + b + core * (a - b)) % SIDE


def remote(src, dst, send_sem, recv_sem, target):
    return pltpu.make_async_remote_copy(
        src_ref=src, dst_ref=dst, send_sem=send_sem, recv_sem=recv_sem,
        device_id=target, device_id_type=MESH,
    )


def wait_bytes(ref, sem):
    pltpu.make_async_copy(ref, ref, sem).wait()


def share(section, z):
    return (section + 2 * (z % 4)) % 8


def dot(a, b):
    return jnp.dot(a, b, preferred_element_type=F32)


def dot_turned(a, b):
    return lax.dot_general(a, b, (((1,), (1,)), ((), ())), preferred_element_type=F32)


LAST = 15
BLOCK = LAYERS * 24
HALF_BLOCK = BLOCK // 2
HALF_LAYERS = LAYERS // 2


def kernel(
    tmpl_ref, split_ref, mb_ref, x_hbm, cot_hbm, down_hbm, up_hbm, order_hbm, grad_down_ref, grad_up_ref,
    layer_at, source, x_ref, cot_ref, order_ref, blocks, work, stage, got,
    inc, turned, part, other, terms, landed, gathered, table,
    far_go, near_go, far_in, near_in, total,
    local_sem, z_send, z_recv, hand_send, hand_recv, pair_send, pair_recv,
    term_send, term_recv, sum_send, sum_recv,
):
    z, x, y, x_lo, section = place()
    core = lax.axis_index("tensor")
    me = seat(x, y)
    odd = z % 2
    targets = [(seat(tx, ty), chip(z, tx, ty)) for tx, ty in plane_steps(x, y)]

    def column(step):
        return chip((z + step + 2 * ZS) % ZS, x, y)

    pair = {"tensor": 1 - core}
    barrier = pltpu.get_barrier_semaphore()
    for _, device in targets:
        pl.semaphore_signal(barrier, inc=1, device_id=device, device_id_type=MESH)
    for step in (1, -1, 2, -2):
        pl.semaphore_signal(barrier, inc=1, device_id=column(step), device_id_type=MESH)
    pl.semaphore_signal(barrier, inc=1, device_id=pair, device_id_type=MESH)

    own = pl.ds(pl.multiple_of(jnp.minimum(share(section, z), 5) * UNIT, UNIT), UNIT)
    loads = [
        pltpu.make_async_copy(down_hbm.at[:, own], blocks.at[0, :, 0], local_sem.at[0]),
        pltpu.make_async_copy(up_hbm.at[:, own], blocks.at[0, :, 1], local_sem.at[1]),
        pltpu.make_async_copy(x_hbm, x_ref, local_sem.at[2]),
        pltpu.make_async_copy(cot_hbm, cot_ref, local_sem.at[3]),
        pltpu.make_async_copy(order_hbm, order_ref, local_sem.at[4]),
    ]
    for load in loads:
        load.start()

    loads[0].wait()
    loads[1].wait()
    pl.semaphore_wait(barrier, PLANE - 1 + 4 + 1)

    def carried(at):
        return share(section, at % ZS) < 6

    def behind(way, distance):
        return (z + ZS - distance) % ZS if way == 0 else (z + distance) % ZS

    def entry_at(way, distance):
        if isinstance(distance, int) and distance in (0, 8):
            return 0 if distance == 0 else LAST
        return jnp.where(distance == 0, 0, 2 * distance - 1 + way)

    def z_copy(way, step, half):
        part = pl.ds(half * HALF_LAYERS, HALF_LAYERS)
        return remote(
            blocks.at[entry_at(way, step - 1), part], blocks.at[entry_at(way, step), part],
            z_send.at[step, way, half], z_recv.at[step, way, half], column(1 if way == 0 else -1),
        )

    def z_each(step, half, action, arriving):
        for way in range(2):
            if isinstance(step, int) and step == 8 and way != half:
                continue

            @pl.when(carried(behind(way, step if arriving else step - 1)))
            def _():
                action(z_copy(way, step, half))

    def z_start(step, half):
        z_each(step, half, lambda copy: copy.start(), False)

    def z_arrived(step, half):
        z_each(step, half, lambda copy: copy.wait_recv(), True)

    def z_sent(step):
        for half in range(2):
            z_each(step, half, lambda copy: copy.wait_send(), False)

    def place_of(entry):
        distance = (entry + 1) // 2
        return jnp.where(entry % 2 == 1, z + ZS - distance, z + distance) % ZS

    def hand_out(entry):
        at = place_of(entry)

        @pl.when(carried(at))
        def _():
            work[...] = blocks[entry]
            for four in range(0, PLANE, 4):
                slots = [(target, slot) for target in range(four, four + 4) for slot in range(2)]
                cut = [work[layer_at[target * 2 + slot]] for target, slot in slots]
                for (target, slot), rows in zip(slots, cut):
                    stage[entry, target, slot] = rows
            unit = (2 * at + x_lo) * 6 + share(section, at)
            got[unit] = stage[entry, me]
            for where, device in targets:
                remote(
                    stage.at[entry, where], got.at[unit], hand_send.at[entry], hand_recv.at[entry], device
                ).start()

    def handed(entry):
        at = place_of(entry)

        @pl.when(carried(at))
        def _():
            wait_bytes(got.at[pl.ds(0, 11)], hand_recv.at[entry])

        @pl.when(jnp.logical_not(carried(at)))
        def _():
            wait_bytes(got.at[pl.ds(0, 12)], hand_recv.at[entry])

    def over(first, last, body):
        def step(index, _):
            body(index)
            return 0

        lax.fori_loop(first, last, step, 0)

    def chunk_of(m, side):
        return (z // 2 + odd + jnp.where(side == 0, m - 1, CHUNKS - m)) % CHUNKS

    def weight(slot, kind, q):
        return got[pl.ds(q * (CHUNK // UNIT), CHUNK // UNIT), slot, kind].reshape(CHUNK, 128)

    def columns(q):
        return pl.ds(pl.multiple_of(q * CHUNK, CHUNK), CHUNK)

    def begin(q):
        cols = columns(q)
        for m in range(4):
            keep = jnp.where(m < live, 1.0, 0.0)
            rows = pl.ds(m * SLAB, SLAB)
            inc[rows, cols] = (cot_ref[rows, cols].astype(F32) * keep).astype(BF16)
        down_zero, down_one, up_zero, up_one = [weight(slot, kind, q) for kind in range(2) for slot in range(2)]
        ahead = dot(x_ref[:, cols], jnp.concatenate([down_zero, down_one], axis=1))
        back = dot(inc[:, cols], jnp.concatenate([up_one, up_zero], axis=1))
        for at, rows in enumerate((ahead[:, :128], ahead[:, 128:], back[:, :128], back[:, 128:])):
            part[pl.ds(at * ROWS, ROWS)] += rows
        part[pl.ds(4 * ROWS, 128)] += lax.dot_general(
            up_zero, down_one, (((0,), (0,)), ((), ())), preferred_element_type=F32
        )

    for half in range(2):
        z_start(1, half)
    for lo in range(2):
        template = tmpl_ref[2 * z + lo]
        firsts = []
        first = jnp.int32(0)
        for s in range(SECTIONS):
            firsts.append(first)
            layer_at[(lo * SECTIONS + s) * 2] = jnp.minimum(first, LAYERS - 1)
            layer_at[(lo * SECTIONS + s) * 2 + 1] = jnp.minimum(first + 1, LAYERS - 1)
            first = first + split_ref[s, template]
        for layer in range(LAYERS):
            at, begins = jnp.int32(0), jnp.int32(0)
            for s in range(1, SECTIONS):
                at = jnp.where(firsts[s] <= layer, s, at)
                begins = jnp.where(firsts[s] <= layer, firsts[s], begins)
            slot = jnp.minimum(layer - begins, 1)
            source[lo * LAYERS + layer] = (lo * SECTIONS + at) * 2 + slot
    live = mb_ref[2 * z + x_lo]
    holds_two = jnp.where(split_ref[section, tmpl_ref[2 * z + x_lo]] > 1, 1.0, 0.0)
    count = jnp.int32(0)
    for relay in range(2 * ZS):
        count = count + mb_ref[relay]

    hand_out(jnp.int32(0))

    def ring_step(step):
        for half in range(2):
            z_arrived(step, half)
            z_start(step + 1, half)
        hand_out(2 * step - 1)
        hand_out(2 * step)

    over(1, 7, ring_step)
    for half in range(2):
        z_arrived(7, half)
        z_start(8, half)
    hand_out(jnp.int32(13))
    hand_out(jnp.int32(14))
    for half in range(2):
        z_arrived(8, half)
    hand_out(jnp.int32(15))

    part[...] = jnp.zeros_like(part)
    for load in loads[2:]:
        load.wait()
    for m in range(1, 5):
        over(0 if m == 1 else 4 * m - 3, min(4 * m + 1, ZS), handed)
        over(0, 2, lambda side: begin(chunk_of(m, side)))

    swap = remote(part, other, pair_send.at[0], pair_recv.at[0], pair)
    swap.start()
    swap.wait()

    def whole(at, rows=ROWS):
        where = pl.ds(at * ROWS, rows)
        return part[where] + other[where]

    through = whole(4, 128)
    through_high = through.astype(BF16)
    through_low = (through - through_high.astype(F32)).astype(BF16)
    value, slope_at_zero = gelu_pair(whole(0))
    act_zero = value.astype(BF16)
    act_zero_t = value.T.astype(BF16)
    pre_one = whole(1) + (dot(act_zero, through_high) + dot(act_zero, through_low))
    value, slope_at_one = gelu_pair(pre_one)
    act_one_t = value.T.astype(BF16)
    slope_one_wide = whole(2) * slope_at_one * holds_two
    slope_one = slope_one_wide.astype(BF16)
    slope_one_t = slope_one_wide.T.astype(BF16)
    back_zero = whole(3) + (dot_turned(slope_one, through_high) + dot_turned(slope_one, through_low))
    slope_zero_t = (back_zero * slope_at_zero).T.astype(BF16)

    def give(q):
        cols = columns(q)
        inputs, incoming = x_ref[:, cols], inc[:, cols]
        input_one = (inputs.astype(F32) + dot_turned(act_zero, weight(0, 1, q))).astype(BF16)
        cot_zero = (incoming.astype(F32) + dot_turned(slope_one, weight(1, 0, q))).astype(BF16)
        turned[:128, :CHUNK] = dot(slope_zero_t, inputs).astype(BF16)
        turned[128:, :CHUNK] = dot(slope_one_t, input_one).astype(BF16)
        turned[:128, CHUNK:] = dot(act_zero_t, cot_zero).astype(BF16)
        turned[128:, CHUNK:] = dot(act_one_t, incoming).astype(BF16)
        sorted_rows = dot_turned(order_ref[...], turned[...]).astype(BF16)
        for slot in range(2):
            terms[q, :, slot] = sorted_rows[:, slot * 128:(slot + 1) * 128].reshape(PLANE, SLAB, 128)
        for where, device in targets:
            remote(terms.at[q, where], landed.at[q, me], term_send.at[q], term_recv.at[q], device).start()

    def add_up(q):
        landed[q, me] = terms[q, me]
        wait_bytes(landed.at[q, pl.ds(0, PLANE - 1)], term_recv.at[q])
        gathered[...] = landed[q].reshape(2 * PLANE, SLAB, 128)
        for two in range(0, LAYERS, 2):
            both = [
                gathered[source[layer]].astype(F32) + gathered[source[LAYERS + layer]].astype(F32)
                for layer in (two, two + 1)
            ]
            for layer, rows in zip((two, two + 1), both):
                table[2 * q, pl.ds(layer * 24, 24)] = rows[:24]
                table[2 * q + 1, pl.ds(layer * 24, 24)] = rows[24:]

    def sum_copy(m, far, way):
        i = 4 - m
        step = (1 + far) * (1 if way == 0 else -1)
        if not far:
            return remote(
                near_go.at[way, i], near_in.at[way, i], sum_send.at[way, i, 0], sum_recv.at[way, i, 0], column(step)
            )
        rows = pl.ds(way * HALF_BLOCK, HALF_BLOCK) if m == 4 else slice(None)
        return remote(
            far_go.at[way, i, rows], far_in.at[way, i, rows], sum_send.at[way, i, 1], sum_recv.at[way, i, 1], column(step)
        )

    def pass_on(m):
        i = 4 - m
        for way in range(2):
            near_go[way, i] = table[behind(1 - way, 2 * m - 1)].astype(BF16)
            sum_copy(m, 0, way).start()
        for way in range(2):
            to = behind(1 - way, 2 * m)
            mine = pl.ds(way * HALF_BLOCK, HALF_BLOCK)
            rest = pl.ds((1 - way) * HALF_BLOCK, HALF_BLOCK)
            if m == 4:
                far_go[way, 0, mine] = table[to, mine].astype(BF16)
            else:
                sum_copy(m + 1, 0, way).wait_recv()
                sum_copy(m + 1, 1, way).wait_recv()
                if m == 3:
                    far_go[way, 1, mine] = (
                        table[to, mine] + near_in[way, 0, mine].astype(F32) + far_in[way, 0, mine].astype(F32)
                    ).astype(BF16)
                    far_go[way, 1, rest] = (table[to, rest] + near_in[way, 0, rest].astype(F32)).astype(BF16)
                else:
                    far_go[way, i] = (
                        table[to] + near_in[way, i - 1].astype(F32) + far_in[way, i - 1].astype(F32)
                    ).astype(BF16)
            sum_copy(m, 1, way).start()

    over(0, 2, lambda side: give(chunk_of(4, side)))
    for m in range(4, 0, -1):
        if m > 1:
            over(0, 2, lambda side: give(chunk_of(m - 1, side)))
        over(0, 2, lambda side: add_up(chunk_of(m, side)))
        pass_on(m)
    result = table[z]
    for way in range(2):
        sum_copy(1, 0, way).wait_recv()
        sum_copy(1, 1, way).wait_recv()
        result = result + near_in[way, 3].astype(F32) + far_in[way, 3].astype(F32)
    total[...] = result / count.astype(F32)
    for layer in range(LAYERS):
        grad_down_ref[layer * 12:layer * 12 + 12] = total[layer * 24:layer * 24 + 12]
        grad_up_ref[layer * 12:layer * 12 + 12] = total[layer * 24 + 12:layer * 24 + 24]

    over(1, 8, z_sent)
    z_sent(8)
    for m in range(1, 5):
        for way in range(2):
            sum_copy(m, 0, way).wait_send()
            sum_copy(m, 1, way).wait_send()

    def left(entry):
        @pl.when(carried(place_of(entry)))
        def _():
            wait_bytes(stage.at[entry, pl.ds(0, PLANE - 1)], hand_send.at[entry])

    over(0, LAST + 1, left)

    def given(q):
        wait_bytes(terms.at[q, pl.ds(0, PLANE - 1)], term_send.at[q])

    over(0, CHUNKS, given)


def row_order():
    order = np.zeros((768, 768), np.float32)
    for lo in range(2):
        for s in range(SECTIONS):
            for near in range(2):
                for kind in range(2):
                    for j in range(12):
                        to = lo * 384 + s * 48 + near * 24 + kind * 12 + j
                        order[to, kind * 384 + (2 * near + lo) * 96 + s * 12 + j] = 1.0
    return order


def local(stashed, cotangent, down_weight, up_weight, layer_split, template_of, mb_count):
    smem, hbm = pl.BlockSpec(memory_space=pltpu.SMEM), pl.BlockSpec(memory_space=pl.ANY)
    dma = pltpu.SemaphoreType.DMA
    grad = jax.ShapeDtypeStruct((LAYERS * 12, 128), F32)
    grad_down, grad_up = pl.pallas_call(
        kernel,
        out_shape=[grad, grad],
        in_specs=[smem] * 3 + [hbm] * 5,
        out_specs=[pl.BlockSpec(memory_space=pltpu.VMEM)] * 2,
        scratch_shapes=[
            pltpu.SMEM((2 * PLANE,), jnp.int32),
            pltpu.SMEM((2 * LAYERS,), jnp.int32),
            pltpu.VMEM((ROWS, HALF), BF16),
            pltpu.VMEM((ROWS, HALF), BF16),
            pltpu.VMEM((768, 768), BF16),
            pltpu.VMEM((ZS, LAYERS, 2, UNIT, 128), BF16),
            pltpu.VMEM((LAYERS, 2, UNIT, 128), BF16),
            pltpu.VMEM((ZS, PLANE, 2, 2, UNIT, 128), BF16),
            pltpu.VMEM((HALF // UNIT, 2, 2, UNIT, 128), BF16),
            pltpu.VMEM((ROWS, HALF), BF16),
            pltpu.VMEM((256, 2 * CHUNK), BF16),
            pltpu.VMEM((4 * ROWS + 128, 128), F32),
            pltpu.VMEM((4 * ROWS + 128, 128), F32),
            pltpu.VMEM((CHUNKS, PLANE, 2, SLAB, 128), BF16),
            pltpu.VMEM((CHUNKS, PLANE, 2, SLAB, 128), BF16),
            pltpu.VMEM((2 * PLANE, SLAB, 128), BF16),
            pltpu.VMEM((ZS, BLOCK, 128), F32),
            pltpu.VMEM((2, 4, BLOCK, 128), BF16),
            pltpu.VMEM((2, 4, BLOCK, 128), BF16),
            pltpu.VMEM((2, 4, BLOCK, 128), BF16),
            pltpu.VMEM((2, 4, BLOCK, 128), BF16),
            pltpu.VMEM((BLOCK, 128), F32),
            dma((5,)), dma((9, 2, 2)), dma((9, 2, 2)), dma((ZS,)), dma((ZS,)), dma((1,)), dma((1,)),
            dma((CHUNKS,)), dma((CHUNKS,)), dma((2, 4, 2)), dma((2, 4, 2)),
        ],
        compiler_params=pltpu.CompilerParams(
            collective_id=1, has_side_effects=True, vmem_limit_bytes=VMEM_LIMIT
        ),
    )(
        template_of, layer_split.T, mb_count, stashed.reshape(ROWS, HALF), cotangent.reshape(ROWS, HALF),
        down_weight[:, 0], up_weight[:, 0], jnp.asarray(row_order(), BF16),
    )
    return grad_down.reshape(LAYERS, 1, 12, 128), grad_up.reshape(LAYERS, 1, 12, 128)


def solution(mesh):
    placed = (
        P("pipe", "section", None, None, "tensor"),
        P("pipe", "section", None, None, "tensor"),
        P(None, "tensor", "pipe", None),
        P(None, "tensor", "pipe", None),
        P(),
        P(),
        P(),
    )
    return jax.shard_map(
        local,
        mesh=mesh,
        in_specs=placed,
        out_specs=(
            P(None, "tensor", ("pipe", "section"), None),
            P(None, "tensor", ("pipe", "section"), None),
        ),
        check_vma=False,
    )
```

```python
import jax
import jax.numpy as jnp
import numpy as np
from jax import lax
from jax.experimental import pallas as pl
from jax.experimental.pallas import tpu as pltpu
from jax.sharding import PartitionSpec as P

MESH = pl.DeviceIdType.MESH
F32 = jnp.float32
BF16 = jnp.bfloat16

LAYERS = 12
SECTIONS = 8
ZS = 16
SIDE = 4
PLANE = 16
ROWS = 192
HALF = 3072
UNIT = 16
CHUNK = 384
CHUNKS = HALF // CHUNK
SLAB = 48
VMEM_LIMIT = 56 * 2**20

OFFSETS = (
    (2, 2), (1, 0), (0, 1), (2, 1), (1, 2), (3, 0), (0, 3), (2, 3),
    (3, 2), (2, 0), (0, 2), (1, 1), (3, 3), (1, 3), (3, 1),
)

gelu_scale = 0.7978845608028654
gelu_cubic = 0.044715


def gelu_pair(values):
    inner = jnp.tanh(gelu_scale * (values + gelu_cubic * values * values * values))
    value = 0.5 * values * (1.0 + inner)
    slope = 0.5 * (1.0 + inner) + 0.5 * values * (1.0 - inner * inner) * gelu_scale * (
        1.0 + 3.0 * gelu_cubic * values * values
    )
    return value, slope


def place():
    pipe = lax.axis_index("pipe")
    section = lax.axis_index("section")
    z, x_lo = pipe // 2, pipe % 2
    x, y = (section // SIDE) * 2 + x_lo, section % SIDE
    return z, x, y, x_lo, section


def chip(z, x, y):
    return {"pipe": z * 2 + x % 2, "section": (x // 2) * SIDE + y}


def seat(x, y):
    return (x % 2) * SECTIONS + (x // 2) * SIDE + y


def plane_steps(x, y):
    core = lax.axis_index("tensor")
    for a, b in OFFSETS:
        yield (x + a + core * (b - a)) % SIDE, (y + b + core * (a - b)) % SIDE


def remote(src, dst, send_sem, recv_sem, target):
    return pltpu.make_async_remote_copy(
        src_ref=src, dst_ref=dst, send_sem=send_sem, recv_sem=recv_sem,
        device_id=target, device_id_type=MESH,
    )


def wait_bytes(ref, sem):
    pltpu.make_async_copy(ref, ref, sem).wait()


def share(section, z):
    return (section + 2 * (z % 4)) % 8


def dot(a, b):
    return jnp.dot(a, b, preferred_element_type=F32)


def dot_turned(a, b):
    return lax.dot_general(a, b, (((1,), (1,)), ((), ())), preferred_element_type=F32)


LAST = 15
BLOCK = LAYERS * 24
HALF_BLOCK = BLOCK // 2
HALF_LAYERS = LAYERS // 2


def kernel(
    tmpl_ref, split_ref, mb_ref, x_hbm, cot_hbm, down_hbm, up_hbm, order_hbm, grads_ref,
    layer_at, source, x_ref, cot_ref, order_ref, blocks, work, stage, got,
    inc, turned, part, other, terms, landed, gathered, table,
    far_go, near_go, far_in, near_in, total,
    local_sem, z_send, z_recv, hand_send, hand_recv, pair_send, pair_recv,
    term_send, term_recv, sum_send, sum_recv,
):
    z, x, y, x_lo, section = place()
    core = lax.axis_index("tensor")
    me = seat(x, y)
    odd = z % 2
    targets = [(seat(tx, ty), chip(z, tx, ty)) for tx, ty in plane_steps(x, y)]

    def column(step):
        return chip((z + step + 2 * ZS) % ZS, x, y)

    pair = {"tensor": 1 - core}
    barrier = pltpu.get_barrier_semaphore()
    for _, device in targets:
        pl.semaphore_signal(barrier, inc=1, device_id=device, device_id_type=MESH)
    for step in (1, -1, 2, -2):
        pl.semaphore_signal(barrier, inc=1, device_id=column(step), device_id_type=MESH)
    pl.semaphore_signal(barrier, inc=1, device_id=pair, device_id_type=MESH)

    own = pl.ds(pl.multiple_of(jnp.minimum(share(section, z), 5) * UNIT, UNIT), UNIT)
    loads = [
        pltpu.make_async_copy(down_hbm.at[:, own], blocks.at[0, :, 0], local_sem.at[0]),
        pltpu.make_async_copy(up_hbm.at[:, own], blocks.at[0, :, 1], local_sem.at[1]),
        pltpu.make_async_copy(x_hbm, x_ref, local_sem.at[2]),
        pltpu.make_async_copy(cot_hbm, cot_ref, local_sem.at[3]),
        pltpu.make_async_copy(order_hbm, order_ref, local_sem.at[4]),
    ]
    for load in loads:
        load.start()

    loads[0].wait()
    loads[1].wait()
    pl.semaphore_wait(barrier, PLANE - 1 + 4 + 1)

    def carried(at):
        return share(section, at % ZS) < 6

    def behind(way, distance):
        return (z + ZS - distance) % ZS if way == 0 else (z + distance) % ZS

    def entry_at(way, distance):
        if isinstance(distance, int) and distance in (0, 8):
            return 0 if distance == 0 else LAST
        return jnp.where(distance == 0, 0, 2 * distance - 1 + way)

    def z_copy(way, step, half):
        part = pl.ds(half * HALF_LAYERS, HALF_LAYERS)
        return remote(
            blocks.at[entry_at(way, step - 1), part], blocks.at[entry_at(way, step), part],
            z_send.at[step, way, half], z_recv.at[step, way, half], column(1 if way == 0 else -1),
        )

    def z_each(step, half, action, arriving):
        for way in range(2):
            if isinstance(step, int) and step == 8 and way != half:
                continue

            @pl.when(carried(behind(way, step if arriving else step - 1)))
            def _():
                action(z_copy(way, step, half))

    def z_start(step, half):
        z_each(step, half, lambda copy: copy.start(), False)

    def z_arrived(step, half):
        z_each(step, half, lambda copy: copy.wait_recv(), True)

    def z_sent(step):
        for half in range(2):
            z_each(step, half, lambda copy: copy.wait_send(), False)

    def place_of(entry):
        distance = (entry + 1) // 2
        return jnp.where(entry % 2 == 1, z + ZS - distance, z + distance) % ZS

    def hand_out(entry):
        at = place_of(entry)

        @pl.when(carried(at))
        def _():
            work[...] = blocks[entry]
            for four in range(0, PLANE, 4):
                slots = [(target, slot) for target in range(four, four + 4) for slot in range(2)]
                cut = [work[layer_at[target * 2 + slot]] for target, slot in slots]
                for (target, slot), rows in zip(slots, cut):
                    stage[entry, target, slot] = rows
            unit = (2 * at + x_lo) * 6 + share(section, at)
            got[unit] = stage[entry, me]
            for where, device in targets:
                remote(
                    stage.at[entry, where], got.at[unit], hand_send.at[entry], hand_recv.at[entry], device
                ).start()

    def handed(entry):
        at = place_of(entry)

        @pl.when(carried(at))
        def _():
            wait_bytes(got.at[pl.ds(0, 11)], hand_recv.at[entry])

        @pl.when(jnp.logical_not(carried(at)))
        def _():
            wait_bytes(got.at[pl.ds(0, 12)], hand_recv.at[entry])

    def over(first, last, body):
        def step(index, _):
            body(index)
            return 0

        lax.fori_loop(first, last, step, 0)

    def chunk_of(m, side):
        return (z // 2 + odd + jnp.where(side == 0, m - 1, CHUNKS - m)) % CHUNKS

    def weight(slot, kind, q):
        return got[pl.ds(q * (CHUNK // UNIT), CHUNK // UNIT), slot, kind].reshape(CHUNK, 128)

    def columns(q):
        return pl.ds(pl.multiple_of(q * CHUNK, CHUNK), CHUNK)

    def begin(q):
        cols = columns(q)
        for m in range(4):
            keep = jnp.where(m < live, 1.0, 0.0)
            rows = pl.ds(m * SLAB, SLAB)
            inc[rows, cols] = (cot_ref[rows, cols].astype(F32) * keep).astype(BF16)
        down_zero, down_one, up_zero, up_one = [weight(slot, kind, q) for kind in range(2) for slot in range(2)]
        ahead = dot(x_ref[:, cols], jnp.concatenate([down_zero, down_one], axis=1))
        back = dot(inc[:, cols], jnp.concatenate([up_one, up_zero], axis=1))
        for at, rows in enumerate((ahead[:, :128], ahead[:, 128:], back[:, :128], back[:, 128:])):
            part[pl.ds(at * ROWS, ROWS)] += rows
        part[pl.ds(4 * ROWS, 128)] += lax.dot_general(
            up_zero, down_one, (((0,), (0,)), ((), ())), preferred_element_type=F32
        )

    for half in range(2):
        z_start(1, half)
    for lo in range(2):
        template = tmpl_ref[2 * z + lo]
        firsts = []
        first = jnp.int32(0)
        for s in range(SECTIONS):
            firsts.append(first)
            layer_at[(lo * SECTIONS + s) * 2] = jnp.minimum(first, LAYERS - 1)
            layer_at[(lo * SECTIONS + s) * 2 + 1] = jnp.minimum(first + 1, LAYERS - 1)
            first = first + split_ref[s, template]
        for layer in range(LAYERS):
            at, begins = jnp.int32(0), jnp.int32(0)
            for s in range(1, SECTIONS):
                at = jnp.where(firsts[s] <= layer, s, at)
                begins = jnp.where(firsts[s] <= layer, firsts[s], begins)
            slot = jnp.minimum(layer - begins, 1)
            source[lo * LAYERS + layer] = (lo * SECTIONS + at) * 2 + slot
    live = mb_ref[2 * z + x_lo]
    holds_two = jnp.where(split_ref[section, tmpl_ref[2 * z + x_lo]] > 1, 1.0, 0.0)
    count = jnp.int32(0)
    for relay in range(2 * ZS):
        count = count + mb_ref[relay]

    hand_out(jnp.int32(0))

    def ring_step(step):
        for half in range(2):
            z_arrived(step, half)
            z_start(step + 1, half)
        hand_out(2 * step - 1)
        hand_out(2 * step)

    over(1, 7, ring_step)
    for half in range(2):
        z_arrived(7, half)
        z_start(8, half)
    hand_out(jnp.int32(13))
    hand_out(jnp.int32(14))
    for half in range(2):
        z_arrived(8, half)
    hand_out(jnp.int32(15))

    part[...] = jnp.zeros_like(part)
    for load in loads[2:]:
        load.wait()
    for m in range(1, 5):
        over(0 if m == 1 else 4 * m - 3, min(4 * m + 1, ZS), handed)
        over(0, 2, lambda side: begin(chunk_of(m, side)))

    swap = remote(part, other, pair_send.at[0], pair_recv.at[0], pair)
    swap.start()
    swap.wait()

    def whole(at, rows=ROWS):
        where = pl.ds(at * ROWS, rows)
        return part[where] + other[where]

    through = whole(4, 128)
    through_high = through.astype(BF16)
    through_low = (through - through_high.astype(F32)).astype(BF16)
    value, slope_at_zero = gelu_pair(whole(0))
    act_zero = value.astype(BF16)
    act_zero_t = value.T.astype(BF16)
    pre_one = whole(1) + (dot(act_zero, through_high) + dot(act_zero, through_low))
    value, slope_at_one = gelu_pair(pre_one)
    act_one_t = value.T.astype(BF16)
    slope_one_wide = whole(2) * slope_at_one * holds_two
    slope_one = slope_one_wide.astype(BF16)
    slope_one_t = slope_one_wide.T.astype(BF16)
    back_zero = whole(3) + (dot_turned(slope_one, through_high) + dot_turned(slope_one, through_low))
    slope_zero_t = (back_zero * slope_at_zero).T.astype(BF16)

    def give(q):
        cols = columns(q)
        inputs, incoming = x_ref[:, cols], inc[:, cols]
        input_one = (inputs.astype(F32) + dot_turned(act_zero, weight(0, 1, q))).astype(BF16)
        cot_zero = (incoming.astype(F32) + dot_turned(slope_one, weight(1, 0, q))).astype(BF16)
        turned[:128, :CHUNK] = dot(slope_zero_t, inputs).astype(BF16)
        turned[128:, :CHUNK] = dot(slope_one_t, input_one).astype(BF16)
        turned[:128, CHUNK:] = dot(act_zero_t, cot_zero).astype(BF16)
        turned[128:, CHUNK:] = dot(act_one_t, incoming).astype(BF16)
        sorted_rows = dot_turned(order_ref[...], turned[...]).astype(BF16)
        for slot in range(2):
            terms[q, :, slot] = sorted_rows[:, slot * 128:(slot + 1) * 128].reshape(PLANE, SLAB, 128)
        for where, device in targets:
            remote(terms.at[q, where], landed.at[q, me], term_send.at[q], term_recv.at[q], device).start()

    def add_up(q):
        landed[q, me] = terms[q, me]
        wait_bytes(landed.at[q, pl.ds(0, PLANE - 1)], term_recv.at[q])
        gathered[...] = landed[q].reshape(2 * PLANE, SLAB, 128)
        for two in range(0, LAYERS, 2):
            both = [
                gathered[source[layer]].astype(F32) + gathered[source[LAYERS + layer]].astype(F32)
                for layer in (two, two + 1)
            ]
            for layer, rows in zip((two, two + 1), both):
                table[2 * q, pl.ds(layer * 24, 24)] = rows[:24]
                table[2 * q + 1, pl.ds(layer * 24, 24)] = rows[24:]

    def sum_copy(m, far, way):
        i = 4 - m
        if not far:
            return remote(
                near_go.at[way, i], near_in.at[way, i], sum_send.at[way, i, 0], sum_recv.at[way, i, 0], column(1 - 2 * way)
            )
        rows = pl.ds(way * HALF_BLOCK, HALF_BLOCK) if m == 4 else slice(None)
        return remote(
            far_go.at[way, i, rows], far_in.at[way, i, rows], sum_send.at[way, i, 1], sum_recv.at[way, i, 1],
            column(2 - 4 * way),
        )

    def pass_near(m, way):
        near_go[way, 4 - m] = table[(z + (2 * m - 1) * (1 - 2 * way) + ZS) % ZS].astype(BF16)
        sum_copy(m, 0, way).start()

    def pass_on(m):
        i = 4 - m
        if m > 1:
            for way in range(2):
                pass_near(m, way)
        for way in range(2):
            to = behind(1 - way, 2 * m)
            mine = pl.ds(way * HALF_BLOCK, HALF_BLOCK)
            rest = pl.ds((1 - way) * HALF_BLOCK, HALF_BLOCK)
            if m == 4:
                far_go[way, 0, mine] = table[to, mine].astype(BF16)
            else:
                sum_copy(m + 1, 0, way).wait_recv()
                sum_copy(m + 1, 1, way).wait_recv()
                if m == 3:
                    far_go[way, 1, mine] = (
                        table[to, mine] + near_in[way, 0, mine].astype(F32) + far_in[way, 0, mine].astype(F32)
                    ).astype(BF16)
                    far_go[way, 1, rest] = (table[to, rest] + near_in[way, 0, rest].astype(F32)).astype(BF16)
                else:
                    far_go[way, i] = (
                        table[to] + near_in[way, i - 1].astype(F32) + far_in[way, i - 1].astype(F32)
                    ).astype(BF16)
            sum_copy(m, 1, way).start()

    def turn(m, i):
        return (i + 1 + odd) % 2 if m == 1 else i

    over(0, 2, lambda side: give(chunk_of(4, side)))
    for m in range(4, 1, -1):
        over(0, 2, lambda i: give(chunk_of(m - 1, turn(m - 1, i))))
        over(0, 2, lambda side: add_up(chunk_of(m, side)))
        pass_on(m)
    add_up(chunk_of(1, 1 - odd))
    pass_near(1, 1 - odd)
    pass_on(1)
    add_up(chunk_of(1, odd))
    pass_near(1, odd)
    result = table[z]
    for way in range(2):
        sum_copy(1, 0, way).wait_recv()
        sum_copy(1, 1, way).wait_recv()
        result = result + near_in[way, 3].astype(F32) + far_in[way, 3].astype(F32)
    total[...] = result / count.astype(F32)
    for layer in range(LAYERS):
        grads_ref[0, layer * 12:layer * 12 + 12] = total[layer * 24:layer * 24 + 12]
        grads_ref[1, layer * 12:layer * 12 + 12] = total[layer * 24 + 12:layer * 24 + 24]

    over(1, 8, z_sent)
    z_sent(8)
    for m in range(1, 5):
        for way in range(2):
            sum_copy(m, 0, way).wait_send()
            sum_copy(m, 1, way).wait_send()

    def left(entry):
        @pl.when(carried(place_of(entry)))
        def _():
            wait_bytes(stage.at[entry, pl.ds(0, PLANE - 1)], hand_send.at[entry])

    over(0, LAST + 1, left)

    def given(q):
        wait_bytes(terms.at[q, pl.ds(0, PLANE - 1)], term_send.at[q])

    over(0, CHUNKS, given)


def row_order():
    order = np.zeros((768, 768), np.float32)
    for lo in range(2):
        for s in range(SECTIONS):
            for near in range(2):
                for kind in range(2):
                    for j in range(12):
                        to = lo * 384 + s * 48 + near * 24 + kind * 12 + j
                        order[to, kind * 384 + (2 * near + lo) * 96 + s * 12 + j] = 1.0
    return order


def local(stashed, cotangent, down_weight, up_weight, layer_split, template_of, mb_count):
    smem, hbm = pl.BlockSpec(memory_space=pltpu.SMEM), pl.BlockSpec(memory_space=pl.ANY)
    dma = pltpu.SemaphoreType.DMA
    grads = pl.pallas_call(
        kernel,
        out_shape=jax.ShapeDtypeStruct((2, LAYERS * 12, 128), F32),
        in_specs=[smem] * 3 + [hbm] * 5,
        out_specs=pl.BlockSpec(memory_space=pltpu.VMEM),
        scratch_shapes=[
            pltpu.SMEM((2 * PLANE,), jnp.int32),
            pltpu.SMEM((2 * LAYERS,), jnp.int32),
            pltpu.VMEM((ROWS, HALF), BF16),
            pltpu.VMEM((ROWS, HALF), BF16),
            pltpu.VMEM((768, 768), BF16),
            pltpu.VMEM((ZS, LAYERS, 2, UNIT, 128), BF16),
            pltpu.VMEM((LAYERS, 2, UNIT, 128), BF16),
            pltpu.VMEM((ZS, PLANE, 2, 2, UNIT, 128), BF16),
            pltpu.VMEM((HALF // UNIT, 2, 2, UNIT, 128), BF16),
            pltpu.VMEM((ROWS, HALF), BF16),
            pltpu.VMEM((256, 2 * CHUNK), BF16),
            pltpu.VMEM((4 * ROWS + 128, 128), F32),
            pltpu.VMEM((4 * ROWS + 128, 128), F32),
            pltpu.VMEM((CHUNKS, PLANE, 2, SLAB, 128), BF16),
            pltpu.VMEM((CHUNKS, PLANE, 2, SLAB, 128), BF16),
            pltpu.VMEM((2 * PLANE, SLAB, 128), BF16),
            pltpu.VMEM((ZS, BLOCK, 128), F32),
            pltpu.VMEM((2, 4, BLOCK, 128), BF16),
            pltpu.VMEM((2, 4, BLOCK, 128), BF16),
            pltpu.VMEM((2, 4, BLOCK, 128), BF16),
            pltpu.VMEM((2, 4, BLOCK, 128), BF16),
            pltpu.VMEM((BLOCK, 128), F32),
            dma((5,)), dma((9, 2, 2)), dma((9, 2, 2)), dma((ZS,)), dma((ZS,)), dma((1,)), dma((1,)),
            dma((CHUNKS,)), dma((CHUNKS,)), dma((2, 4, 2)), dma((2, 4, 2)),
        ],
        compiler_params=pltpu.CompilerParams(
            collective_id=1, has_side_effects=True, vmem_limit_bytes=VMEM_LIMIT
        ),
    )(
        template_of, layer_split.T, mb_count, stashed.reshape(ROWS, HALF), cotangent.reshape(ROWS, HALF),
        down_weight[:, 0], up_weight[:, 0], jnp.asarray(row_order(), BF16),
    )
    return grads[0].reshape(LAYERS, 1, 12, 128), grads[1].reshape(LAYERS, 1, 12, 128)


def solution(mesh):
    placed = (
        P("pipe", "section", None, None, "tensor"),
        P("pipe", "section", None, None, "tensor"),
        P(None, "tensor", "pipe", None),
        P(None, "tensor", "pipe", None),
        P(),
        P(),
        P(),
    )
    return jax.shard_map(
        local,
        mesh=mesh,
        in_specs=placed,
        out_specs=(
            P(None, "tensor", ("pipe", "section"), None),
            P(None, "tensor", ("pipe", "section"), None),
        ),
        check_vma=False,
    )
```

```python
import jax
import jax.numpy as jnp
import numpy as np
from jax import lax
from jax.experimental import pallas as pl
from jax.experimental.pallas import tpu as pltpu
from jax.sharding import PartitionSpec as P

MESH = pl.DeviceIdType.MESH
F32 = jnp.float32
BF16 = jnp.bfloat16

LAYERS = 12
SECTIONS = 8
ZS = 16
SIDE = 4
PLANE = 16
ROWS = 192
HALF = 3072
UNIT = 16
CHUNK = 384
CHUNKS = HALF // CHUNK
SLAB = 48
VMEM_LIMIT = 56 * 2**20

OFFSETS = (
    (2, 2), (1, 0), (0, 1), (2, 1), (1, 2), (3, 0), (0, 3), (2, 3),
    (3, 2), (2, 0), (0, 2), (1, 1), (3, 3), (1, 3), (3, 1),
)

gelu_scale = 0.7978845608028654
gelu_cubic = 0.044715


def gelu_pair(values):
    inner = jnp.tanh(gelu_scale * (values + gelu_cubic * values * values * values))
    value = 0.5 * values * (1.0 + inner)
    slope = 0.5 * (1.0 + inner) + 0.5 * values * (1.0 - inner * inner) * gelu_scale * (
        1.0 + 3.0 * gelu_cubic * values * values
    )
    return value, slope


def place():
    pipe = lax.axis_index("pipe")
    section = lax.axis_index("section")
    z, x_lo = pipe // 2, pipe % 2
    x, y = (section // SIDE) * 2 + x_lo, section % SIDE
    return z, x, y, x_lo, section


def chip(z, x, y):
    return {"pipe": z * 2 + x % 2, "section": (x // 2) * SIDE + y}


def seat(x, y):
    return (x % 2) * SECTIONS + (x // 2) * SIDE + y


def plane_steps(x, y):
    core = lax.axis_index("tensor")
    for a, b in OFFSETS:
        yield (x + a + core * (b - a)) % SIDE, (y + b + core * (a - b)) % SIDE


def remote(src, dst, send_sem, recv_sem, target):
    return pltpu.make_async_remote_copy(
        src_ref=src, dst_ref=dst, send_sem=send_sem, recv_sem=recv_sem,
        device_id=target, device_id_type=MESH,
    )


def wait_bytes(ref, sem):
    pltpu.make_async_copy(ref, ref, sem).wait()


def share(section, z):
    return (section + 2 * (z % 4)) % 8


def dot(a, b):
    return jnp.dot(a, b, preferred_element_type=F32)


def dot_turned(a, b):
    return lax.dot_general(a, b, (((1,), (1,)), ((), ())), preferred_element_type=F32)


LAST = 15
SPARE = 8
BLOCK = LAYERS * 24
HALF_BLOCK = BLOCK // 2
HALF_LAYERS = LAYERS // 2


def kernel(
    tmpl_ref, split_ref, mb_ref, x_hbm, cot_hbm, down_hbm, up_hbm, order_hbm, grads_ref,
    layer_at, source, x_ref, cot_ref, order_ref, blocks, work, stage, got,
    inc, turned, part, other, terms, landed, gathered, table,
    far_go, near_go, far_in, near_in, total,
    local_sem, z_send, z_recv, hand_send, hand_recv, pair_send, pair_recv,
    term_send, term_recv, sum_send, sum_recv,
):
    z, x, y, x_lo, section = place()
    core = lax.axis_index("tensor")
    me = seat(x, y)
    odd = z % 2
    targets = [(seat(tx, ty), chip(z, tx, ty)) for tx, ty in plane_steps(x, y)]

    def column(step):
        return chip((z + step + 2 * ZS) % ZS, x, y)

    pair = {"tensor": 1 - core}

    own = pl.ds(pl.multiple_of(jnp.minimum(share(section, z), 5) * UNIT, UNIT), UNIT)
    loads = [
        pltpu.make_async_copy(down_hbm.at[:, own], blocks.at[0, :, 0], local_sem.at[0]),
        pltpu.make_async_copy(up_hbm.at[:, own], blocks.at[0, :, 1], local_sem.at[1]),
        pltpu.make_async_copy(x_hbm, x_ref, local_sem.at[2]),
        pltpu.make_async_copy(cot_hbm, cot_ref, local_sem.at[3]),
        pltpu.make_async_copy(order_hbm, order_ref, local_sem.at[4]),
    ]
    for load in loads:
        load.start()

    barrier = pltpu.get_barrier_semaphore()
    for _, device in targets:
        pl.semaphore_signal(barrier, inc=1, device_id=device, device_id_type=MESH)
    for step in (1, -1, 2, -2):
        pl.semaphore_signal(barrier, inc=1, device_id=column(step), device_id_type=MESH)
    pl.semaphore_signal(barrier, inc=1, device_id=pair, device_id_type=MESH)

    for lo in range(2):
        template = tmpl_ref[2 * z + lo]
        firsts = []
        first = jnp.int32(0)
        for s in range(SECTIONS):
            firsts.append(first)
            layer_at[(lo * SECTIONS + s) * 2] = jnp.minimum(first, LAYERS - 1)
            layer_at[(lo * SECTIONS + s) * 2 + 1] = jnp.minimum(first + 1, LAYERS - 1)
            first = first + split_ref[s, template]
        for layer in range(LAYERS):
            at, begins = jnp.int32(0), jnp.int32(0)
            for s in range(1, SECTIONS):
                at = jnp.where(firsts[s] <= layer, s, at)
                begins = jnp.where(firsts[s] <= layer, firsts[s], begins)
            slot = jnp.minimum(layer - begins, 1)
            source[lo * LAYERS + layer] = (lo * SECTIONS + at) * 2 + slot
    live = mb_ref[2 * z + x_lo]
    holds_two = jnp.where(split_ref[section, tmpl_ref[2 * z + x_lo]] > 1, 1.0, 0.0)
    count = jnp.int32(0)
    for relay in range(2 * ZS):
        count = count + mb_ref[relay]

    loads[0].wait()
    loads[1].wait()
    pl.semaphore_wait(barrier, PLANE - 1 + 4 + 1)

    def carried(at):
        return share(section, at % ZS) < 6

    def behind(way, distance):
        return (z + ZS - distance) % ZS if way == 0 else (z + distance) % ZS

    def entry_at(way, distance):
        if isinstance(distance, int) and distance in (0, 8):
            return 0 if distance == 0 else LAST
        return jnp.where(distance == 0, 0, 2 * distance - 1 + way)

    def z_copy(way, step, half):
        part = pl.ds(half * HALF_LAYERS, HALF_LAYERS)
        return remote(
            blocks.at[entry_at(way, step - 1), part], blocks.at[entry_at(way, step), part],
            z_send.at[step, way, half], z_recv.at[step, way, half], column(1 if way == 0 else -1),
        )

    def z_each(step, half, action, arriving):
        for way in range(2):
            if isinstance(step, int) and step == 8 and way != half:
                continue

            @pl.when(carried(behind(way, step if arriving else step - 1)))
            def _():
                action(z_copy(way, step, half))

    def z_start(step, half):
        z_each(step, half, lambda copy: copy.start(), False)

    def z_arrived(step, half):
        z_each(step, half, lambda copy: copy.wait_recv(), True)

    def z_sent(step):
        for half in range(2):
            z_each(step, half, lambda copy: copy.wait_send(), False)

    def place_of(entry):
        distance = (entry + 1) // 2
        return jnp.where(entry % 2 == 1, z + ZS - distance, z + distance) % ZS

    def hand_out(entry):
        at = place_of(entry)

        @pl.when(carried(at))
        def _():
            work[...] = blocks[entry]
            for four in range(0, PLANE, 4):
                slots = [(target, slot) for target in range(four, four + 4) for slot in range(2)]
                cut = [work[layer_at[target * 2 + slot]] for target, slot in slots]
                for (target, slot), rows in zip(slots, cut):
                    stage[entry, target, slot] = rows
            unit = (2 * at + x_lo) * 6 + share(section, at)
            got[unit] = stage[entry, me]
            for where, device in targets:
                remote(
                    stage.at[entry, where], got.at[unit], hand_send.at[entry], hand_recv.at[entry], device
                ).start()

    def handed(entry):
        at = place_of(entry)

        @pl.when(carried(at))
        def _():
            wait_bytes(got.at[pl.ds(0, 11)], hand_recv.at[entry])

        @pl.when(jnp.logical_not(carried(at)))
        def _():
            wait_bytes(got.at[pl.ds(0, 12)], hand_recv.at[entry])

    def over(first, last, body):
        def step(index, _):
            body(index)
            return 0

        lax.fori_loop(first, last, step, 0)

    def chunk_of(m, side):
        return (z // 2 + odd + jnp.where(side == 0, m - 1, CHUNKS - m)) % CHUNKS

    def weight(slot, kind, q):
        return got[pl.ds(q * (CHUNK // UNIT), CHUNK // UNIT), slot, kind].reshape(CHUNK, 128)

    def columns(q):
        return pl.ds(pl.multiple_of(q * CHUNK, CHUNK), CHUNK)

    def begin(q):
        cols = columns(q)
        for m in range(4):
            keep = jnp.where(m < live, 1.0, 0.0)
            rows = pl.ds(m * SLAB, SLAB)
            inc[rows, cols] = (cot_ref[rows, cols].astype(F32) * keep).astype(BF16)
        down_zero, down_one, up_zero, up_one = [weight(slot, kind, q) for kind in range(2) for slot in range(2)]
        ahead = dot(x_ref[:, cols], jnp.concatenate([down_zero, down_one], axis=1))
        back = dot(inc[:, cols], jnp.concatenate([up_one, up_zero], axis=1))
        for at, rows in enumerate((ahead[:, :128], ahead[:, 128:], back[:, :128], back[:, 128:])):
            part[pl.ds(at * ROWS, ROWS)] += rows
        part[pl.ds(4 * ROWS, 128)] += lax.dot_general(
            up_zero, down_one, (((0,), (0,)), ((), ())), preferred_element_type=F32
        )

    for half in range(2):
        z_start(1, half)
    hand_out(jnp.int32(0))

    def ring_step(step):
        for half in range(2):
            z_arrived(step, half)
            z_start(step + 1, half)
        hand_out(2 * step - 1)
        hand_out(2 * step)

    over(1, 7, ring_step)
    for half in range(2):
        z_arrived(7, half)
        z_start(8, half)
    hand_out(jnp.int32(13))
    hand_out(jnp.int32(14))
    for half in range(2):
        z_arrived(8, half)
    hand_out(jnp.int32(15))

    part[...] = jnp.zeros_like(part)
    for load in loads[2:]:
        load.wait()
    for m in range(1, 5):
        over(0 if m == 1 else 4 * m - 3, 4 * m + 1 if m < 4 else LAST, handed)
        if m < 4:
            over(0, 2, lambda side: begin(chunk_of(m, side)))
    begin(chunk_of(4, odd))
    handed(jnp.int32(LAST))
    begin(chunk_of(4, 1 - odd))

    swap = remote(part, other, pair_send.at[0], pair_recv.at[0], pair)
    swap.start()
    swap.wait()

    def whole(at, rows=ROWS):
        where = pl.ds(at * ROWS, rows)
        return part[where] + other[where]

    through = whole(4, 128)
    through_high = through.astype(BF16)
    through_low = (through - through_high.astype(F32)).astype(BF16)
    value, slope_at_zero = gelu_pair(whole(0))
    act_zero = value.astype(BF16)
    act_zero_t = value.T.astype(BF16)
    pre_one = whole(1) + (dot(act_zero, through_high) + dot(act_zero, through_low))
    value, slope_at_one = gelu_pair(pre_one)
    act_one_t = value.T.astype(BF16)
    slope_one_wide = whole(2) * slope_at_one * holds_two
    slope_one = slope_one_wide.astype(BF16)
    slope_one_t = slope_one_wide.T.astype(BF16)
    back_zero = whole(3) + (dot_turned(slope_one, through_high) + dot_turned(slope_one, through_low))
    slope_zero_t = (back_zero * slope_at_zero).T.astype(BF16)

    def give(q):
        cols = columns(q)
        inputs, incoming = x_ref[:, cols], inc[:, cols]
        input_one = (inputs.astype(F32) + dot_turned(act_zero, weight(0, 1, q))).astype(BF16)
        cot_zero = (incoming.astype(F32) + dot_turned(slope_one, weight(1, 0, q))).astype(BF16)
        turned[:128, :CHUNK] = dot(slope_zero_t, inputs).astype(BF16)
        turned[128:, :CHUNK] = dot(slope_one_t, input_one).astype(BF16)
        turned[:128, CHUNK:] = dot(act_zero_t, cot_zero).astype(BF16)
        turned[128:, CHUNK:] = dot(act_one_t, incoming).astype(BF16)
        sorted_rows = dot_turned(order_ref[...], turned[...]).astype(BF16)
        for slot in range(2):
            terms[q, :, slot] = sorted_rows[:, slot * 128:(slot + 1) * 128].reshape(PLANE, SLAB, 128)
        for where, device in targets:
            remote(terms.at[q, where], landed.at[q, me], term_send.at[q], term_recv.at[q], device).start()

    def add_up(q):
        landed[q, me] = terms[q, me]
        wait_bytes(landed.at[q, pl.ds(0, PLANE - 1)], term_recv.at[q])
        gathered[...] = landed[q].reshape(2 * PLANE, SLAB, 128)
        for two in range(0, LAYERS, 2):
            both = [
                gathered[source[layer]].astype(F32) + gathered[source[LAYERS + layer]].astype(F32)
                for layer in (two, two + 1)
            ]
            for layer, rows in zip((two, two + 1), both):
                table[2 * q, pl.ds(layer * 24, 24)] = rows[:24]
                table[2 * q + 1, pl.ds(layer * 24, 24)] = rows[24:]

    def sum_copy(m, far, way):
        i = 4 - m
        if not far:
            return remote(
                near_go.at[way, i], near_in.at[way, i], sum_send.at[way, i, 0], sum_recv.at[way, i, 0], column(1 - 2 * way)
            )
        rows = pl.ds(way * HALF_BLOCK, HALF_BLOCK) if m == 4 else slice(None)
        return remote(
            far_go.at[way, i, rows], far_in.at[way, i, rows], sum_send.at[way, i, 1], sum_recv.at[way, i, 1],
            column(2 - 4 * way),
        )

    def pass_near(m, way):
        near_go[way, 4 - m] = table[(z + (2 * m - 1) * (1 - 2 * way) + ZS) % ZS].astype(BF16)
        sum_copy(m, 0, way).start()

    def pass_on(m):
        i = 4 - m
        if m > 1:
            for way in range(2):
                pass_near(m, way)
        for way in range(2):
            to = behind(1 - way, 2 * m)
            mine = pl.ds(way * HALF_BLOCK, HALF_BLOCK)
            rest = pl.ds((1 - way) * HALF_BLOCK, HALF_BLOCK)
            if m == 4:
                far_go[way, 0, mine] = table[to, mine].astype(BF16)
            else:
                sum_copy(m + 1, 0, way).wait_recv()
                sum_copy(m + 1, 1, way).wait_recv()
                if m == 3:
                    far_go[way, 1, mine] = (
                        table[to, mine] + near_in[way, 0, mine].astype(F32) + far_in[way, 0, mine].astype(F32)
                    ).astype(BF16)
                    far_go[way, 1, rest] = (table[to, rest] + near_in[way, 0, rest].astype(F32)).astype(BF16)
                else:
                    far_go[way, i] = (
                        table[to] + near_in[way, i - 1].astype(F32) + far_in[way, i - 1].astype(F32)
                    ).astype(BF16)
            sum_copy(m, 1, way).start()

    def turn(m, i):
        return (i + 1 + odd) % 2 if m == 1 else i

    over(0, 2, lambda side: give(chunk_of(4, side)))
    for m in range(4, 1, -1):
        over(0, 2, lambda i: give(chunk_of(m - 1, turn(m - 1, i))))
        over(0, 2, lambda side: add_up(chunk_of(m, side)))
        pass_on(m)
    add_up(chunk_of(1, 1 - odd))
    pass_near(1, 1 - odd)
    pass_on(1)
    add_up(chunk_of(1, odd))
    pass_near(1, odd)
    result = table[z]
    for way in range(2):
        sum_copy(1, 0, way).wait_recv()
        sum_copy(1, 1, way).wait_recv()
        result = result + near_in[way, 3].astype(F32) + far_in[way, 3].astype(F32)
    total[:BLOCK] = result / count.astype(F32)
    for layer in range(LAYERS):
        grads_ref[0, layer * 12:layer * 12 + 12] = total[layer * 24:layer * 24 + 12]
        grads_ref[1, layer * 12:layer * 12 + 12] = total[layer * 24 + 12:layer * 24 + 24]

    over(1, 8, z_sent)
    z_sent(8)
    for m in range(1, 5):
        for way in range(2):
            sum_copy(m, 0, way).wait_send()
            sum_copy(m, 1, way).wait_send()

    def left(entry):
        @pl.when(carried(place_of(entry)))
        def _():
            wait_bytes(stage.at[entry, pl.ds(0, PLANE - 1)], hand_send.at[entry])

    over(0, LAST + 1, left)

    def given(q):
        wait_bytes(terms.at[q, pl.ds(0, PLANE - 1)], term_send.at[q])

    over(0, CHUNKS, given)


def row_order():
    order = np.zeros((768, 768), np.float32)
    for lo in range(2):
        for s in range(SECTIONS):
            for near in range(2):
                for kind in range(2):
                    for j in range(12):
                        to = lo * 384 + s * 48 + near * 24 + kind * 12 + j
                        order[to, kind * 384 + (2 * near + lo) * 96 + s * 12 + j] = 1.0
    return order


def local(stashed, cotangent, down_weight, up_weight, layer_split, template_of, mb_count):
    smem, hbm = pl.BlockSpec(memory_space=pltpu.SMEM), pl.BlockSpec(memory_space=pl.ANY)
    dma = pltpu.SemaphoreType.DMA
    grads = pl.pallas_call(
        kernel,
        out_shape=jax.ShapeDtypeStruct((2, LAYERS * 12 + SPARE, 128), F32),
        in_specs=[smem] * 3 + [hbm] * 5,
        out_specs=pl.BlockSpec(memory_space=pltpu.VMEM),
        scratch_shapes=[
            pltpu.SMEM((2 * PLANE,), jnp.int32),
            pltpu.SMEM((2 * LAYERS,), jnp.int32),
            pltpu.VMEM((ROWS, HALF), BF16),
            pltpu.VMEM((ROWS, HALF), BF16),
            pltpu.VMEM((768, 768), BF16),
            pltpu.VMEM((ZS, LAYERS, 2, UNIT, 128), BF16),
            pltpu.VMEM((LAYERS, 2, UNIT, 128), BF16),
            pltpu.VMEM((ZS, PLANE, 2, 2, UNIT, 128), BF16),
            pltpu.VMEM((HALF // UNIT, 2, 2, UNIT, 128), BF16),
            pltpu.VMEM((ROWS, HALF), BF16),
            pltpu.VMEM((256, 2 * CHUNK), BF16),
            pltpu.VMEM((4 * ROWS + 128, 128), F32),
            pltpu.VMEM((4 * ROWS + 128, 128), F32),
            pltpu.VMEM((CHUNKS, PLANE, 2, SLAB, 128), BF16),
            pltpu.VMEM((CHUNKS, PLANE, 2, SLAB, 128), BF16),
            pltpu.VMEM((2 * PLANE, SLAB, 128), BF16),
            pltpu.VMEM((ZS, BLOCK, 128), F32),
            pltpu.VMEM((2, 4, BLOCK, 128), BF16),
            pltpu.VMEM((2, 4, BLOCK, 128), BF16),
            pltpu.VMEM((2, 4, BLOCK, 128), BF16),
            pltpu.VMEM((2, 4, BLOCK, 128), BF16),
            pltpu.VMEM((BLOCK + SPARE, 128), F32),
            dma((5,)), dma((9, 2, 2)), dma((9, 2, 2)), dma((ZS,)), dma((ZS,)), dma((1,)), dma((1,)),
            dma((CHUNKS,)), dma((CHUNKS,)), dma((2, 4, 2)), dma((2, 4, 2)),
        ],
        compiler_params=pltpu.CompilerParams(
            collective_id=1, has_side_effects=True, vmem_limit_bytes=VMEM_LIMIT
        ),
    )(
        template_of, layer_split.T, mb_count, stashed.reshape(ROWS, HALF), cotangent.reshape(ROWS, HALF),
        down_weight[:, 0], up_weight[:, 0], jnp.asarray(row_order(), BF16),
    )
    grad_down, grad_up = grads[0, :LAYERS * 12], grads[1, :LAYERS * 12]
    return grad_down.reshape(LAYERS, 1, 12, 128), grad_up.reshape(LAYERS, 1, 12, 128)


def solution(mesh):
    placed = (
        P("pipe", "section", None, None, "tensor"),
        P("pipe", "section", None, None, "tensor"),
        P(None, "tensor", "pipe", None),
        P(None, "tensor", "pipe", None),
        P(),
        P(),
        P(),
    )
    return jax.shard_map(
        local,
        mesh=mesh,
        in_specs=placed,
        out_specs=(
            P(None, "tensor", ("pipe", "section"), None),
            P(None, "tensor", ("pipe", "section"), None),
        ),
        check_vma=False,
    )
```
